256 devices in a mesh: cell: 64 (over z_hi, y, x), orb: 4 (over z_lo, core).
Axes of the slice: x: 4, y: 4, z: 8 (z_hi: 4, z_lo: 2; z = z_hi * 2 + z_lo), core: 2. Of those that a mesh axis runs over, the one named last changes fastest.
Arguments:
- orbitals: bfloat16 [256, 663552], P('orb', 'cell'), may hold values from -6 to 6
- panels: bfloat16 [128, 663552], P('orb', 'cell'), may hold values from -0.01953125 to 0.01953125
- stiffness: bfloat16 [343, 343], replicated, may hold values from -0.3 to 2.5
- potential: float32 [343, 3072], P(None, 'cell'), may hold values from -1 to 3
- connectivity: int32 [343, 3072], P(None, 'cell'), may hold values from 0 to 12095, as said below
- boundary: int32 [110592], P('cell'), may hold values from 0 to 10367, as said below
Outputs:
- applied: bfloat16 [256, 663552], P('orb', 'cell')
- projected: float32 [128, 256], P('cell', 'orb')
The draws below stay inside these ranges and needn't reach their ends.
Inputs may be any that keep to these rules, and one draw needn't show every extreme that they name: `connectivity`: A partition's entries number its own 10368 nodes below 10368 and, from 10368 on, the 1728 nodes it shares with the next partition, in the order of that partition's boundary entries; every number is used by some cell. `boundary`: A partition's 1728 entries are distinct numbers of its own nodes.
All inputs are finite; a program needn't handle non-finite values.
Results may differ from the reference program's by a relative error of at most 0.0028.
Values may be sent and summed in bfloat16 or wider, within the bound.
A program may use at most 64 MiB of HBM per device.

```python
import jax
import jax.numpy as jnp
from jax import lax

BLOCK = 256
PANEL = 128
NPE = 343
CX = 12
CY = 4
CELLS_DEV = 48
CELLS = 3072
NODES_DEV = 10368
GHOST = 1728
NODES = 663552
N_CELL = 64


def node_order(key):
    parts = CELLS // CELLS_DEV
    keys = jax.vmap(lambda index: jax.random.fold_in(key, index))(jnp.arange(parts))
    return jax.vmap(lambda sub: jax.random.permutation(sub, NODES_DEV))(keys).astype(jnp.int32)


def draw_connectivity(key, part):
    orders = node_order(key)
    span_x = 6 * CX
    span_y = 6 * CY
    cell_ids = jnp.arange(CELLS_DEV)
    cell_x = cell_ids // CY
    cell_y = cell_ids % CY
    local = jnp.arange(NPE)
    along_z = local // 49
    along_x = local // 7 % 7
    along_y = local % 7
    node_x = (6 * cell_x[None, :] + along_x[:, None]) % span_x
    node_y = (6 * cell_y[None, :] + along_y[:, None]) % span_y
    node_z = jnp.broadcast_to(along_z[:, None], node_x.shape)
    natural = (jnp.minimum(node_z, 5) * span_x + node_x) * span_y + node_y
    owned = orders[:, natural]
    ghost = NODES_DEV + node_x * span_y + node_y
    result = jnp.where(node_z[None] < 6, owned, ghost[None])
    return result.transpose(1, 0, 2).reshape(NPE, CELLS).astype(jnp.int32)


def draw_boundary(key, part):
    orders = node_order(key)
    return orders[:, :GHOST].reshape(-1).astype(jnp.int32)


def draw_stiffness(key, part):
    key = jax.random.fold_in(key, 5)
    first, second = jax.random.split(key)
    diagonal = 1.5 + jax.random.uniform(first, (NPE,), jnp.float32)
    others = 0.06 * jnp.clip(jax.random.normal(second, (NPE, NPE), jnp.float32), -5.0, 5.0)
    eye_mask = jnp.arange(NPE)[:, None] == jnp.arange(NPE)[None, :]
    return jnp.where(eye_mask, diagonal[:, None], others).astype(jnp.bfloat16)


def with_spikes(drawn, key, source, target, shards_of, factor):
    def block_of(dim):
        return (jnp.arange(drawn.shape[dim]) // (drawn.shape[dim] // shards_of)).reshape((-1,) + (1,) * (drawn.ndim - 1 - dim))

    one_side = jax.random.permutation(key, shards_of)[block_of(target)]
    other_side = (block_of(target) + shards_of // 2) % shards_of
    return jnp.where((block_of(source) == one_side) | (block_of(source) == other_side), factor * drawn, drawn)


def block_scale(rng, extent, cuts, least, high):
    def one(position, shards_of):
        draws = jax.random.uniform(jax.random.fold_in(jax.random.fold_in(rng, 6), position), (shards_of,), jnp.float32, least / len(cuts), high / len(cuts))
        return jnp.repeat(jnp.exp(draws), extent[position] // shards_of).reshape((-1,) + (1,) * (len(extent) - position - 1))

    level = one(*cuts[0])
    for cut in cuts[1:]:
        level = level * one(*cut)
    return level


def centred(own_key, shape, deviation, most, shards=(), kind=jnp.bfloat16):
    entries = jax.random.normal(own_key, shape, jnp.float32) * deviation
    if len(shards) > 0:
        entries = block_scale(own_key, shape, shards, -0.22, 0.18) * entries
    return jnp.clip(entries, min=-most, max=most).astype(kind)


def heavy_noise(stream_key, dims, scale, most, shards, heavy, dtype=jnp.bfloat16):
    values = scale * jax.random.normal(stream_key, dims, jnp.float32)
    if shards:
        values = values * block_scale(stream_key, dims, shards, -0.22, 0.18)
    return jnp.clip(with_spikes(values, jax.random.fold_in(stream_key, 3), *heavy), -most, most).astype(dtype)


def setup_inputs(seed: int = 0) -> dict:
    streams_of = jax.random.split(jax.random.key(seed), 7)
    orbitals = centred(streams_of[0], (BLOCK, NODES), 1.0, 6.0, ((0, 4), (1, 64)))
    panels = heavy_noise(streams_of[1], (PANEL, NODES), NODES ** -0.5, 0.01953125, ((0, 4), (1, 64)), (1, 0, 64, 4.0))
    stiffness = draw_stiffness(jax.random.fold_in(streams_of[6], 71), 0)
    potential = jnp.clip(-1.0 + 4.0 * jax.random.uniform(streams_of[3], (NPE, CELLS), jnp.float32) ** block_scale(streams_of[3], (NPE, CELLS), ((1, 64),), -0.2, 0.2), -1.0, 3.0)
    connectivity = draw_connectivity(jax.random.fold_in(streams_of[6], 71), 0)
    boundary = draw_boundary(jax.random.fold_in(streams_of[6], 71), 0)
    return dict(orbitals=orbitals, panels=panels, stiffness=stiffness, potential=potential, connectivity=connectivity, boundary=boundary)


def reference(orbitals, panels, stiffness, potential, connectivity, boundary):
    parts = N_CELL
    x_parts = orbitals.reshape(BLOCK, parts, NODES_DEV).transpose(1, 0, 2)
    p_parts = panels.reshape(PANEL, parts, NODES_DEV).transpose(1, 0, 2)
    c_parts = connectivity.reshape(NPE, parts, CELLS_DEV).transpose(1, 0, 2)
    v_parts = potential.reshape(NPE, parts, CELLS_DEV).transpose(1, 0, 2)
    b_parts = boundary.reshape(parts, GHOST)
    edges = jax.vmap(lambda values, index: jnp.take(values, index, axis=1))(x_parts, b_parts)
    ghosts = jnp.concatenate([edges[1:], jnp.zeros_like(edges[:1])], axis=0)
    stiff = stiffness.astype(jnp.float32)

    def step(carry, items):
        incoming, total = carry
        own, ghost_vals, conn, pot, bound, pan = items
        local = jnp.concatenate([own, ghost_vals], axis=1)
        gathered = jnp.take(local, conn, axis=1)
        element_out = jnp.einsum("ij,bjc->bic", stiff, gathered.astype(jnp.float32))
        element_out = element_out + pot[None] * gathered.astype(jnp.float32)
        assembled = jnp.zeros((BLOCK, NODES_DEV + GHOST), jnp.float32).at[:, conn].add(element_out)
        owned = assembled[:, :NODES_DEV].at[:, bound].add(incoming)
        applied = owned.astype(jnp.bfloat16)
        total = total + jnp.dot(pan, applied.T, preferred_element_type=jnp.float32)
        return (assembled[:, NODES_DEV:], total), applied

    start = (jnp.zeros((BLOCK, GHOST), jnp.float32), jnp.zeros((PANEL, BLOCK), jnp.float32))
    (last, projected), applied = lax.scan(step, start, (x_parts, ghosts, c_parts, v_parts, b_parts, p_parts))
    applied = applied.transpose(1, 0, 2).reshape(BLOCK, parts * NODES_DEV)
    return applied, projected
```

```python
import jax
import jax.numpy as jnp
from jax import lax
from jax.experimental import pallas as pl
from jax.experimental.pallas import tpu as pltpu
from jax.sharding import PartitionSpec as P

ORB = 64
NPE = 343
ROWS = 344
DEEP = 384
CELLS = 48
HALF_CELLS = 24
OWN = 10368
GHOST = 1728
LOCAL = OWN + GHOST
PANELS = 128
N_CELL = 64
LOW = 5248
HALF_GHOST = 864
PACKED = LOW + HALF_GHOST
BATCH = 8
MIB = 2**20
ANY = pl.BlockSpec(memory_space=pl.ANY)
VMEM = pl.BlockSpec(memory_space=pltpu.VMEM)
SMEM = pl.BlockSpec(memory_space=pltpu.SMEM)
MESH = pl.DeviceIdType.MESH
F32 = jnp.float32
BF16 = jnp.bfloat16


def places():
    cell = lax.axis_index("cell")
    orb = lax.axis_index("orb")
    core = lax.rem(orb, 2)
    peer = {"orb": orb + 1 - 2 * core}
    before = {"cell": lax.rem(cell + N_CELL - 1, N_CELL)}
    after = {"cell": lax.rem(cell + 1, N_CELL)}
    return cell, core, peer, before, after


def greet(signalled, waits):
    barrier = pltpu.get_barrier_semaphore()
    for device in signalled:
        pl.semaphore_signal(barrier, inc=1, device_id=device, device_id_type=MESH)
    pl.semaphore_wait(barrier, waits)


def remote(src, dst, send, recv, device):
    return pltpu.make_async_remote_copy(
        src_ref=src, dst_ref=dst, send_sem=send, recv_sem=recv, device_id=device, device_id_type=MESH
    )


X_CHUNKS = 3
X_WIDE = OWN // X_CHUNKS
G_CHUNKS = 3
G_ROWS = HALF_GHOST // G_CHUNKS


def collect_kernel(
    orb_ref, bound_ref, out_ref, x, table, rows, leaving, landed, local_sem, xs_sem, xr_sem, gs_sem, gr_sem, fs_sem, fr_sem, out_sem
):
    cell, core, peer, before, after = places()
    mine = pl.ds(pl.multiple_of(core * ORB, ORB), ORB)
    columns = [pl.ds(c * X_WIDE, X_WIDE) for c in range(X_CHUNKS)]
    own = [pltpu.make_async_copy(orb_ref.at[:, s], x.at[mine, s], local_sem.at[c]) for c, s in enumerate(columns)]
    for copy in own:
        copy.start()
    greet([peer, after], 2)
    given = [remote(orb_ref.at[:, s], x.at[mine, s], xs_sem.at[c], xr_sem.at[c], peer) for c, s in enumerate(columns)]
    for copy in given:
        copy.start()
    stored = []
    for c in range(X_CHUNKS):
        own[c].wait()
        given[c].wait_recv()

        def turn(b, carry, c=c):
            at = pl.multiple_of(c * X_WIDE + b * 128, 128)
            table[pl.ds(at, 128), :] = x[:, pl.ds(at, 128)].astype(F32).T
            return carry

        lax.fori_loop(0, X_WIDE // 128, turn, 0)
        part = pl.ds(c * X_WIDE, X_WIDE)
        stored.append(pltpu.make_async_copy(table.at[part], out_ref.at[part], out_sem.at[c]))
        stored[-1].start()
    base = core * HALF_GHOST
    sent = []
    for g in range(G_CHUNKS):

        def pick(t, carry, g=g):
            at = g * G_ROWS + t * 16
            for j in range(16):
                rows[pl.ds(j, 1), :] = table[pl.ds(bound_ref[base + at + j], 1), :]
            leaving[pl.ds(pl.multiple_of(at, 16), 16), :] = rows[...].astype(BF16)
            return carry

        lax.fori_loop(0, G_ROWS // 16, pick, 0)
        src = pl.ds(g * G_ROWS, G_ROWS)
        dst = pl.ds(pl.multiple_of(base + g * G_ROWS, 16), G_ROWS)
        sent.append(remote(leaving.at[src], landed.at[dst], gs_sem.at[g], gr_sem.at[g], before))
        sent[-1].start()
    passed = []
    for g in range(G_CHUNKS):
        sent[g].wait_recv()
        dst = pl.ds(pl.multiple_of(base + g * G_ROWS, 16), G_ROWS)
        passed.append(remote(landed.at[dst], landed.at[dst], fs_sem.at[g], fr_sem.at[g], peer))
        passed[-1].start()
    for copy in passed:
        copy.wait_recv()
    inner = cell < N_CELL - 1
    table[OWN:, :] = jnp.where(inner, landed[...].astype(F32), 0.0)
    part = pl.ds(OWN, GHOST)
    stored.append(pltpu.make_async_copy(table.at[part], out_ref.at[part], out_sem.at[X_CHUNKS]))
    stored[-1].start()
    for copy in given + sent + passed:
        copy.wait_send()
    for copy in stored:
        copy.wait()


def collect(orbitals, boundary):
    dma = pltpu.SemaphoreType.DMA
    return pl.pallas_call(
        collect_kernel,
        out_shape=jax.ShapeDtypeStruct((LOCAL, 2 * ORB), F32),
        in_specs=[ANY, SMEM],
        out_specs=ANY,
        scratch_shapes=[
            pltpu.VMEM((2 * ORB, OWN), BF16),
            pltpu.VMEM((LOCAL, 2 * ORB), F32),
            pltpu.VMEM((16, 2 * ORB), F32),
            pltpu.VMEM((HALF_GHOST, 2 * ORB), BF16),
            pltpu.VMEM((GHOST, 2 * ORB), BF16),
            dma((X_CHUNKS,)),
            dma((X_CHUNKS,)),
            dma((X_CHUNKS,)),
            dma((G_CHUNKS,)),
            dma((G_CHUNKS,)),
            dma((G_CHUNKS,)),
            dma((G_CHUNKS,)),
            dma((X_CHUNKS + 1,)),
        ],
        compiler_params=pltpu.CompilerParams(collective_id=0, has_side_effects=True, vmem_limit_bytes=40 * MIB),
    )(orbitals, boundary)


def element_kernel(conn_ref, conn_vec, pot_ref, stiff_ref, table, own_ref, leave_ref, even, odd, gathered, product, weights, scaled):
    core = lax.rem(lax.axis_index("orb"), 2)
    first = core * HALF_CELLS
    even[...] = jnp.zeros_like(even)
    odd[...] = jnp.zeros_like(odd)
    gathered[NPE:, :] = jnp.zeros((DEEP - NPE, 2 * ORB), F32)
    weights[...] = jnp.zeros_like(weights)
    weights[:NPE, :NPE] = stiff_ref[...]
    scaled[...] = jnp.zeros_like(scaled)
    scaled[:NPE, :CELLS] = pot_ref[...]

    alike = jnp.zeros((1, CELLS), jnp.int32)
    for d in range(1, BATCH):
        same = conn_vec[: NPE - d, :] == conn_vec[d:NPE, :]
        alike = jnp.maximum(alike, jnp.max(same.astype(jnp.int32), axis=0, keepdims=True))
    repeats = jnp.max(alike)

    def element(e):
        for j in range(NPE):
            gathered[pl.ds(j, 1), :] = table[pl.ds(conn_ref[j, e], 1), :]
        full = gathered[...]
        level = jnp.take_along_axis(scaled[...], jnp.full((ROWS, 128), e, jnp.int32), axis=1)
        kinetic = jnp.dot(weights[...], full.astype(BF16), preferred_element_type=F32)
        product[...] = kinetic + level * full[:ROWS, :]

    def spread(t, carry):
        e = first + t
        element(e)
        for b, start in enumerate(range(0, NPE, BATCH)):
            total = odd if b % 2 else even
            js = range(start, min(NPE, start + BATCH))
            at = [conn_ref[j, e] for j in js]
            sums = [total[pl.ds(i, 1), :] + product[pl.ds(j, 1), :] for i, j in zip(at, js)]
            for i, value in zip(at, sums):
                total[pl.ds(i, 1), :] = value
        return carry

    def spread_singly(t, carry):
        e = first + t
        element(e)

        def add(j, inner):
            i = conn_ref[j, e]
            even[pl.ds(i, 1), :] = even[pl.ds(i, 1), :] + product[pl.ds(j, 1), :]
            return inner

        lax.fori_loop(0, NPE, add, 0)
        return carry

    @pl.when(repeats == 0)
    def _():
        lax.fori_loop(0, HALF_CELLS, spread, 0)

    @pl.when(repeats != 0)
    def _():
        lax.fori_loop(0, HALF_CELLS, spread_singly, 0)

    lane = lax.broadcasted_iota(jnp.int32, (16, 128), 1)

    def pack(low, high, to):
        a = even[low, :] + odd[low, :]
        b = even[high, :] + odd[high, :]
        zero = jnp.where(lane < ORB, a, pltpu.roll(b, ORB, 1))
        one = jnp.where(lane < ORB, pltpu.roll(a, ORB, 1), b)
        own_ref[to, :] = jnp.where(core == 0, zero, one)
        leave_ref[to, :] = jnp.where(core == 0, one, zero).astype(BF16)

    def pack_nodes(r, carry):
        at = pl.multiple_of(r * 16, 16)
        pack(pl.ds(at, 16), pl.ds(LOW + at, 16), pl.ds(at, 16))
        return carry

    def pack_ghosts(r, carry):
        at = pl.multiple_of(r * 16, 16)
        pack(pl.ds(OWN + at, 16), pl.ds(OWN + HALF_GHOST + at, 16), pl.ds(LOW + at, 16))
        return carry

    lax.fori_loop(0, LOW // 16, pack_nodes, 0)
    lax.fori_loop(0, HALF_GHOST // 16, pack_ghosts, 0)


def elements(connectivity, potential, stiffness, table):
    return pl.pallas_call(
        element_kernel,
        out_shape=(jax.ShapeDtypeStruct((PACKED, 128), F32), jax.ShapeDtypeStruct((PACKED, 128), BF16)),
        in_specs=[SMEM, VMEM, VMEM, VMEM, VMEM],
        out_specs=(VMEM, VMEM),
        scratch_shapes=[
            pltpu.VMEM((LOCAL, 128), F32),
            pltpu.VMEM((LOCAL, 128), F32),
            pltpu.VMEM((DEEP, 128), F32),
            pltpu.VMEM((ROWS, 128), F32),
            pltpu.VMEM((ROWS, DEEP), BF16),
            pltpu.VMEM((ROWS, 128), F32),
        ],
        compiler_params=pltpu.CompilerParams(vmem_limit_bytes=56 * MIB),
    )(connectivity, connectivity, potential, stiffness, table)


def swap_kernel(own_ref, leave_ref, got_ref, in_ref, edge, other, leaving, sem, ss, sr):
    cell, core, peer, before, after = places()
    mine = pltpu.make_async_copy(own_ref.at[pl.ds(LOW, HALF_GHOST)], edge, sem)
    mine.start()
    greet([peer, before], 2)
    ghosts = remote(leave_ref.at[pl.ds(LOW, HALF_GHOST)], other, ss.at[0], sr.at[0], peer)
    ghosts.start()
    nodes = remote(leave_ref.at[pl.ds(0, LOW)], got_ref, ss.at[1], sr.at[1], peer)
    nodes.start()
    mine.wait()
    ghosts.wait_recv()
    leaving[...] = (edge[...] + other[...].astype(F32)).astype(BF16)
    shared = remote(leaving, in_ref, ss.at[2], sr.at[2], after)
    shared.start()
    nodes.wait_recv()
    shared.wait_recv()
    for copy in (ghosts, nodes, shared):
        copy.wait_send()


def swap(own, leave):
    return pl.pallas_call(
        swap_kernel,
        out_shape=(jax.ShapeDtypeStruct((LOW, 128), BF16), jax.ShapeDtypeStruct((HALF_GHOST, 128), BF16)),
        in_specs=[ANY, ANY],
        out_specs=(ANY, ANY),
        scratch_shapes=[
            pltpu.VMEM((HALF_GHOST, 128), F32),
            pltpu.VMEM((HALF_GHOST, 128), BF16),
            pltpu.VMEM((HALF_GHOST, 128), BF16),
            pltpu.SemaphoreType.DMA,
            pltpu.SemaphoreType.DMA((3,)),
            pltpu.SemaphoreType.DMA((3,)),
        ],
        compiler_params=pltpu.CompilerParams(collective_id=1, has_side_effects=True, vmem_limit_bytes=16 * MIB),
    )(own, leave)


def finish_kernel(bound_ref, own_ref, got_ref, in_ref, panels_ref, applied_ref, term_ref, nodes, ghosts):
    inner = lax.axis_index("cell") > 0

    def join(r, carry):
        at = pl.multiple_of(r * 128, 128)
        both = own_ref[pl.ds(at, 128), :] + got_ref[pl.ds(at, 128), :].astype(F32)
        nodes[pl.ds(at, 128), :] = both
        nodes[pl.ds(LOW + at, 128), :] = pltpu.roll(both, ORB, 1)
        return carry

    lax.fori_loop(0, LOW // 128, join, 0)
    edge = jnp.where(inner, in_ref[...].astype(F32), 0.0)
    ghosts[:HALF_GHOST, :] = edge
    ghosts[HALF_GHOST:, :] = pltpu.roll(edge, ORB, 1)

    def add(t, carry):
        at = t * 16
        to = [bound_ref[at + j] for j in range(16)]
        base = pl.multiple_of(at, 16)
        sums = [nodes[pl.ds(i, 1), :] + ghosts[pl.ds(base + j, 1), :] for j, i in enumerate(to)]
        for i, value in zip(to, sums):
            nodes[pl.ds(i, 1), :] = value
        return carry

    lax.fori_loop(0, GHOST // 16, add, 0)
    wide = 384
    term_ref[...] = jnp.zeros_like(term_ref)

    def turn(b, carry):
        at = pl.multiple_of(b * wide, 128)
        rounded = nodes[pl.ds(at, wide), :].astype(BF16)
        term_ref[...] += jnp.dot(panels_ref[:, pl.ds(at, wide)], rounded, preferred_element_type=F32)
        applied_ref[:, pl.ds(at, wide)] = nodes[pl.ds(at, wide), :].T[:ORB, :].astype(BF16)
        return carry

    lax.fori_loop(0, OWN // wide, turn, 0)


def finish(boundary, own, got, edge, panels):
    return pl.pallas_call(
        finish_kernel,
        out_shape=(jax.ShapeDtypeStruct((ORB, OWN), BF16), jax.ShapeDtypeStruct((PANELS, 128), F32)),
        in_specs=[SMEM, VMEM, VMEM, VMEM, VMEM],
        out_specs=(VMEM, VMEM),
        scratch_shapes=[pltpu.VMEM((2 * LOW, 128), F32), pltpu.VMEM((GHOST, 128), F32)],
        compiler_params=pltpu.CompilerParams(vmem_limit_bytes=56 * MIB),
    )(boundary, own, got, edge, panels)


def total_kernel(term_ref, out_ref, held, sem, ss, sr):
    cell = lax.axis_index("cell")
    barrier = pltpu.get_barrier_semaphore()

    def hail(d, carry):
        to = lax.rem(cell + d, N_CELL)
        pl.semaphore_signal(barrier, inc=1, device_id={"cell": to}, device_id_type=MESH)
        return carry

    lax.fori_loop(1, N_CELL, hail, 0)
    mine = pltpu.make_async_copy(term_ref.at[cell], held.at[0], sem)
    mine.start()
    pl.semaphore_wait(barrier, N_CELL - 1)

    def send(d, carry):
        to = lax.rem(cell + d, N_CELL)
        remote(term_ref.at[to], held.at[d], ss, sr, {"cell": to}).start()
        return carry

    lax.fori_loop(1, N_CELL, send, 0)
    rest = pl.ds(1, N_CELL - 1)
    every = remote(term_ref.at[rest], held.at[rest], ss, sr, {"cell": lax.rem(cell + 1, N_CELL)})
    mine.wait()
    every.wait()
    out_ref[...] = jnp.sum(held[...], axis=0)


def total(terms):
    return pl.pallas_call(
        total_kernel,
        out_shape=jax.ShapeDtypeStruct((2, 128), F32),
        in_specs=[VMEM],
        out_specs=VMEM,
        scratch_shapes=[
            pltpu.VMEM((N_CELL, 2, 128), F32),
            pltpu.SemaphoreType.DMA,
            pltpu.SemaphoreType.DMA,
            pltpu.SemaphoreType.DMA,
        ],
        compiler_params=pltpu.CompilerParams(collective_id=2, has_side_effects=True),
    )(terms)


def shards(orbitals, panels, stiffness, potential, connectivity, boundary):
    every_panel = lax.all_gather(panels, "orb", axis=0, tiled=True)
    table = collect(orbitals, boundary)
    own, leave = elements(connectivity, potential, stiffness, table)
    got, edge = swap(own, leave)
    applied, term = finish(boundary, own, got, edge, every_panel)
    block = total(term.reshape(N_CELL, PANELS // N_CELL, 128))
    return applied, block[:, :ORB]


def solution(mesh):
    return jax.shard_map(
        shards,
        mesh=mesh,
        in_specs=(
            P("orb", "cell"),
            P("orb", "cell"),
            P(),
            P(None, "cell"),
            P(None, "cell"),
            P("cell"),
        ),
        out_specs=(P("orb", "cell"), P("cell", "orb")),
        check_vma=False,
    )
```

```python
import jax
import jax.numpy as jnp
from jax import lax
from jax.experimental import pallas as pl
from jax.experimental.pallas import tpu as pltpu
from jax.sharding import PartitionSpec as P

ORB = 64
NPE = 343
ROWS = 344
DEEP = 384
CELLS = 48
HALF_CELLS = 24
OWN = 10368
GHOST = 1728
LOCAL = OWN + GHOST
PANELS = 128
N_CELL = 64
LOW = 5248
HALF_GHOST = 864
PACKED = LOW + HALF_GHOST
BATCH = 8
VMEM_LIMIT = 63 * 2**20
NODE_PACK = 656
GHOST_PACK = 432
TEAM = 4
ANY = pl.BlockSpec(memory_space=pltpu.HBM)
VMEM = pl.BlockSpec(memory_space=pltpu.VMEM)
SMEM = pl.BlockSpec(memory_space=pltpu.SMEM)
MESH = pl.DeviceIdType.MESH
F32 = jnp.float32
BF16 = jnp.bfloat16


def places():
    cell = lax.axis_index("cell")
    orb = lax.axis_index("orb")
    core = lax.rem(orb, 2)
    peer = {"orb": orb + 1 - 2 * core}
    before = {"cell": lax.rem(cell + N_CELL - 1, N_CELL)}
    after = {"cell": lax.rem(cell + 1, N_CELL)}
    return cell, core, peer, before, after


def greet(signalled, waits):
    barrier = pltpu.get_barrier_semaphore()
    for device in signalled:
        pl.semaphore_signal(barrier, inc=1, device_id=device, device_id_type=MESH)
    pl.semaphore_wait(barrier, waits)


def remote(src, dst, send, recv, device):
    return pltpu.make_async_remote_copy(
        src_ref=src, dst_ref=dst, send_sem=send, recv_sem=recv, device_id=device, device_id_type=MESH
    )


X_CHUNKS = 3
X_WIDE = OWN // X_CHUNKS
X_TURN = 1152
G_CHUNKS = 3
G_TURN = 96
G_ROWS = HALF_GHOST // G_CHUNKS


def collect_kernel(
    orb_ref, bound_ref, out_ref, x, table, rows, leaving, landed, local_sem, xs_sem, xr_sem, gs_sem, gr_sem, fs_sem, fr_sem, out_sem
):
    cell, core, peer, before, after = places()
    mine = pl.ds(pl.multiple_of(core * ORB, ORB), ORB)
    columns = [pl.ds(c * X_WIDE, X_WIDE) for c in range(X_CHUNKS)]
    own = [pltpu.make_async_copy(orb_ref.at[:, s], x.at[mine, s], local_sem.at[c]) for c, s in enumerate(columns)]
    for copy in own:
        copy.start()
    inner = cell < N_CELL - 1
    sends = cell > 0
    barrier = pltpu.get_barrier_semaphore()
    pl.semaphore_signal(barrier, inc=1, device_id=peer, device_id_type=MESH)

    @pl.when(inner)
    def _():
        pl.semaphore_signal(barrier, inc=1, device_id=after, device_id_type=MESH)

    pl.semaphore_wait(barrier, jnp.where(sends, 2, 1))
    given = [remote(orb_ref.at[:, s], x.at[mine, s], xs_sem.at[c], xr_sem.at[c], peer) for c, s in enumerate(columns)]
    for copy in given:
        copy.start()
    stored = []
    for c in range(X_CHUNKS):
        own[c].wait()
        given[c].wait_recv()

        def turn(b, carry, c=c):
            at = pl.multiple_of(c * X_WIDE + b * X_TURN, 128)
            table[pl.ds(at, X_TURN), :] = x[:, pl.ds(at, X_TURN)].T.astype(F32)
            return carry

        lax.fori_loop(0, X_WIDE // X_TURN, turn, 0)
        part = pl.ds(c * X_WIDE, X_WIDE)
        stored.append(pltpu.make_async_copy(table.at[part], out_ref.at[part], out_sem.at[c]))
        stored[-1].start()
    base = core * HALF_GHOST
    sent, passed = [], []
    for g in range(G_CHUNKS):

        def pick(t, carry, g=g):
            at = g * G_ROWS + t * G_TURN
            for j in range(G_TURN):
                rows[pl.ds(j, 1), :] = table[pl.ds(bound_ref[base + at + j], 1), :]
            leaving[pl.ds(pl.multiple_of(at, 16), G_TURN), :] = rows[...].astype(BF16)
            return carry

        src = pl.ds(g * G_ROWS, G_ROWS)
        dst = pl.ds(pl.multiple_of(base + g * G_ROWS, 16), G_ROWS)
        sent.append(remote(leaving.at[src], landed.at[dst], gs_sem.at[g], gr_sem.at[g], before))
        passed.append(remote(landed.at[dst], landed.at[dst], fs_sem.at[g], fr_sem.at[g], peer))

        @pl.when(sends)
        def _(pick=pick, g=g):
            lax.fori_loop(0, G_ROWS // G_TURN, pick, 0)
            sent[g].start()

    part = pl.ds(OWN, GHOST)
    stored.append(pltpu.make_async_copy(table.at[part], out_ref.at[part], out_sem.at[X_CHUNKS]))

    @pl.when(inner)
    def _():
        for g in range(G_CHUNKS):
            sent[g].wait_recv()
            passed[g].start()
        for copy in passed:
            copy.wait_recv()
        table[OWN:, :] = landed[...].astype(F32)
        for copy in passed:
            copy.wait_send()

    @pl.when(jnp.logical_not(inner))
    def _():
        table[OWN:, :] = jnp.zeros((GHOST, 2 * ORB), F32)

    stored[-1].start()
    for copy in given:
        copy.wait_send()

    @pl.when(sends)
    def _():
        for copy in sent:
            copy.wait_send()

    for copy in stored:
        copy.wait()


def collect(orbitals, boundary):
    dma = pltpu.SemaphoreType.DMA
    return pl.pallas_call(
        collect_kernel,
        out_shape=jax.ShapeDtypeStruct((LOCAL, 2 * ORB), F32),
        in_specs=[ANY, SMEM],
        out_specs=ANY,
        scratch_shapes=[
            pltpu.VMEM((2 * ORB, OWN), BF16),
            pltpu.VMEM((LOCAL, 2 * ORB), F32),
            pltpu.VMEM((G_TURN, 2 * ORB), F32),
            pltpu.VMEM((HALF_GHOST, 2 * ORB), BF16),
            pltpu.VMEM((GHOST, 2 * ORB), BF16),
            dma((X_CHUNKS,)),
            dma((X_CHUNKS,)),
            dma((X_CHUNKS,)),
            dma((G_CHUNKS,)),
            dma((G_CHUNKS,)),
            dma((G_CHUNKS,)),
            dma((G_CHUNKS,)),
            dma((X_CHUNKS + 1,)),
        ],
        compiler_params=pltpu.CompilerParams(collective_id=0, has_side_effects=True, vmem_limit_bytes=VMEM_LIMIT),
    )(orbitals, boundary)


def element_kernel(conn_ref, conn_vec, pot_ref, stiff_ref, table_ref, own_ref, leave_ref, table, leaving, even, odd, near, early, weights, scaled, scaled_t, sems):
    fetch = pltpu.make_async_copy(table_ref, table, sems.at[6])
    fetch.start()
    core = lax.rem(lax.axis_index("orb"), 2)
    first = core * HALF_CELLS
    even[...] = jnp.zeros_like(even)
    odd[...] = jnp.zeros_like(odd)
    near[:, NPE:, :] = jnp.zeros((TEAM, DEEP - NPE, 128), F32)
    weights[...] = jnp.zeros_like(weights)
    weights[:NPE, :NPE] = stiff_ref[...]
    scaled[...] = jnp.zeros_like(scaled)
    scaled[:CELLS, :NPE] = pot_ref[...]
    levels = scaled[...].T
    scaled_t[...] = levels

    alike = jnp.zeros((CELLS, 1), jnp.int32)
    for d in range(1, BATCH):
        same = conn_vec[:, : NPE - d] == conn_vec[:, d:NPE]
        alike = jnp.maximum(alike, jnp.max(same.astype(jnp.int32), axis=1, keepdims=True))
    repeats = jnp.max(alike)
    fetch.wait()

    def index(t, j):
        return conn_ref[(first + t) * NPE + j]

    def gather(t, js):
        for h in range(TEAM):
            for j in js:
                near[h, pl.ds(j, 1), :] = table[pl.ds(index(t + h, j), 1), :]

    def multiply(t):
        full = jnp.concatenate([near[h] for h in range(TEAM)], axis=1).astype(BF16)
        out = jnp.dot(weights[...], full, preferred_element_type=F32)
        for h in range(TEAM):
            level = jnp.take_along_axis(scaled_t[:ROWS, :], jnp.full((ROWS, 128), first + t + h, jnp.int32), axis=1)
            early[h] = out[:, h * 128 : h * 128 + 128] + level * near[h, :ROWS, :]

    def scatter(t, js):
        for h in range(TEAM):
            total = odd if h % 2 else even
            at = [index(t + h, j) for j in js]
            sums = [total[pl.ds(i, 1), :] + early[h, pl.ds(j, 1), :] for i, j in zip(at, js)]
            for i, value in zip(at, sums):
                total[pl.ds(i, 1), :] = value

    batches = [range(b, min(NPE, b + BATCH)) for b in range(0, NPE, BATCH)]

    def team(u, carry):
        t = TEAM * u
        for js in batches:
            gather(t, js)
            scatter(jnp.maximum(t - TEAM, 0), js)

        @pl.when(t >= 0)
        def _():
            multiply(t)

        return carry

    @pl.when(repeats == 0)
    def _():
        early[...] = jnp.zeros_like(early)
        lax.fori_loop(0, HALF_CELLS // TEAM, team, 0)
        for js in batches:
            scatter(HALF_CELLS - TEAM, js)

    @pl.when(repeats != 0)
    def _():
        def one(u, carry):
            def pick(j, inner):
                gather(TEAM * u, [j])
                return inner

            def add(j, inner):
                for h in range(TEAM):
                    i = index(TEAM * u + h, j)
                    even[pl.ds(i, 1), :] = even[pl.ds(i, 1), :] + early[h, pl.ds(j, 1), :]
                return inner

            lax.fori_loop(0, NPE, pick, 0)
            multiply(TEAM * u)
            lax.fori_loop(0, NPE, add, 0)
            return carry

        lax.fori_loop(0, HALF_CELLS // TEAM, one, 0)

    puts = []

    def pack(low, high, to, count):
        lane = lax.broadcasted_iota(jnp.int32, (count, 128), 1)
        straight = (lane < ORB) == (core == 0)
        low, high, to = (pl.ds(s, count) for s in (low, high, to))
        a = even[low, :] + odd[low, :]
        b = even[high, :] + odd[high, :]
        kept = jnp.where(lane < ORB, a, b)
        moved = pltpu.roll(jnp.where(lane < ORB, b, a), ORB, 1)
        table[to, :] = jnp.where(straight, kept, moved)
        leaving[to, :] = jnp.where(straight, moved, kept).astype(BF16)

    def put(start, count):
        part = pl.ds(start, count)
        puts.append(pltpu.make_async_copy(table.at[part], own_ref.at[part], sems.at[len(puts)]))
        puts[-1].start()
        puts.append(pltpu.make_async_copy(leaving.at[part], leave_ref.at[part], sems.at[len(puts)]))
        puts[-1].start()

    def pack_ghosts(r, carry):
        at = pl.multiple_of(r * GHOST_PACK, 16)
        pack(OWN + at, OWN + HALF_GHOST + at, LOW + at, GHOST_PACK)
        return carry

    def pack_nodes(r, carry):
        at = pl.multiple_of(r * NODE_PACK, 16)
        pack(at, LOW + at, at, NODE_PACK)
        return carry

    lax.fori_loop(0, HALF_GHOST // GHOST_PACK, pack_ghosts, 0)
    put(LOW, HALF_GHOST)
    turns = LOW // NODE_PACK
    lax.fori_loop(0, turns // 2, pack_nodes, 0)
    put(0, LOW // 2)
    lax.fori_loop(turns // 2, turns, pack_nodes, 0)
    put(LOW // 2, LOW // 2)
    for copy in puts:
        copy.wait()


def elements(connectivity, potential, stiffness, table):
    return pl.pallas_call(
        element_kernel,
        out_shape=(jax.ShapeDtypeStruct((PACKED, 128), F32), jax.ShapeDtypeStruct((PACKED, 128), BF16)),
        in_specs=[SMEM, VMEM, VMEM, VMEM, ANY],
        out_specs=(ANY, ANY),
        scratch_shapes=[
            pltpu.VMEM((LOCAL, 128), F32),
            pltpu.VMEM((PACKED, 128), BF16),
            pltpu.VMEM((LOCAL, 128), F32),
            pltpu.VMEM((LOCAL, 128), F32),
            pltpu.VMEM((TEAM, DEEP, 128), F32),
            pltpu.VMEM((TEAM, ROWS, 128), F32),
            pltpu.VMEM((ROWS, DEEP), BF16),
            pltpu.VMEM((128, DEEP), F32),
            pltpu.VMEM((DEEP, 128), F32),
            pltpu.SemaphoreType.DMA((7,)),
        ],
        compiler_params=pltpu.CompilerParams(vmem_limit_bytes=VMEM_LIMIT),
        cost_estimate=pl.CostEstimate(flops=2 * HALF_CELLS * NPE * NPE * 128, bytes_accessed=60 * 2**20, transcendentals=0),
    )(connectivity.T.reshape(-1), connectivity.T, potential.T, stiffness, table)


def swap_kernel(own_ref, leave_ref, panels_ref, far_ref, got_ref, in_ref, side_ref, edge, other, leaving, sem, ss, sr):
    cell, core, peer, before, after = places()
    mine = pltpu.make_async_copy(own_ref.at[pl.ds(LOW, HALF_GHOST)], edge, sem)
    mine.start()
    inner = cell > 0
    sends = cell < N_CELL - 1
    barrier = pltpu.get_barrier_semaphore()
    pl.semaphore_signal(barrier, inc=1, device_id=peer, device_id_type=MESH)

    @pl.when(inner)
    def _():
        pl.semaphore_signal(barrier, inc=1, device_id=before, device_id_type=MESH)

    pl.semaphore_wait(barrier, jnp.where(sends, 2, 1))
    ghosts = remote(leave_ref.at[pl.ds(LOW, HALF_GHOST)], other, ss.at[0], sr.at[0], peer)
    ghosts.start()
    nodes = remote(leave_ref.at[pl.ds(0, LOW)], got_ref, ss.at[1], sr.at[1], peer)
    nodes.start()
    rows = panels_ref.shape[0]
    near = remote(panels_ref, side_ref.at[pl.ds(0, rows)], ss.at[3], sr.at[3], peer)
    near.start()
    far = remote(far_ref, side_ref.at[pl.ds(rows, rows)], ss.at[4], sr.at[4], peer)
    far.start()
    mine.wait()
    ghosts.wait_recv()
    shared = remote(leaving, in_ref, ss.at[2], sr.at[2], after)

    @pl.when(sends)
    def _():
        leaving[...] = (edge[...] + other[...].astype(F32)).astype(BF16)
        shared.start()

    for copy in (nodes, near, far):
        copy.wait_recv()

    @pl.when(inner)
    def _():
        shared.wait_recv()

    for copy in (ghosts, nodes, near, far):
        copy.wait_send()

    @pl.when(sends)
    def _():
        shared.wait_send()


def swap(own, leave, panels, far):
    rows = panels.shape[0]
    return pl.pallas_call(
        swap_kernel,
        out_shape=(
            jax.ShapeDtypeStruct((LOW, 128), BF16),
            jax.ShapeDtypeStruct((HALF_GHOST, 128), BF16),
            jax.ShapeDtypeStruct((2 * rows, OWN), BF16),
        ),
        in_specs=[ANY, ANY, ANY, ANY],
        out_specs=(ANY, ANY, ANY),
        scratch_shapes=[
            pltpu.VMEM((HALF_GHOST, 128), F32),
            pltpu.VMEM((HALF_GHOST, 128), BF16),
            pltpu.VMEM((HALF_GHOST, 128), BF16),
            pltpu.SemaphoreType.DMA,
            pltpu.SemaphoreType.DMA((5,)),
            pltpu.SemaphoreType.DMA((5,)),
        ],
        compiler_params=pltpu.CompilerParams(collective_id=1, has_side_effects=True, vmem_limit_bytes=VMEM_LIMIT),
    )(own, leave, panels, far)


JOIN = 656
TURN = 1152
PICKS = 16
PICK_TURNS = 9


def finish_kernel(
    bound_ref, own_ref, got_ref, in_ref, mine_ref, far_ref, side_ref, applied_ref, term_ref, own, got, edge, panels, nodes, ghosts, turned, sems
):
    inner = lax.axis_index("cell") > 0
    gets = []
    for h in range(2):
        part = pl.ds(h * LOW // 2, LOW // 2)
        gets.append(pltpu.make_async_copy(own_ref.at[part], own.at[part], sems.at[2 * h]))
        gets.append(pltpu.make_async_copy(got_ref.at[part], got.at[part], sems.at[2 * h + 1]))
    gets.append(pltpu.make_async_copy(in_ref, edge, sems.at[4]))
    for copy in gets:
        copy.start()
    orb = lax.axis_index("orb")
    other, across = orb + 1 - 2 * lax.rem(orb, 2), lax.rem(orb + 2, 4)
    count = mine_ref.shape[0]
    sources = (mine_ref, far_ref, side_ref.at[pl.ds(0, count)], side_ref.at[pl.ds(count, count)])
    rows = (orb, across, other, lax.rem(other + 2, 4))
    parts = []
    for k, (source, row) in enumerate(zip(sources, rows)):
        to = panels.at[pl.ds(pl.multiple_of(row * count, count), count)]
        parts.append(pltpu.make_async_copy(source, to, sems.at[5 + k]))
        parts[-1].start()
    term_ref[...] = jnp.zeros_like(term_ref)

    def join(r, carry):
        at = pl.multiple_of(r * JOIN, 16)
        both = own[pl.ds(at, JOIN), :] + got[pl.ds(at, JOIN), :].astype(F32)
        nodes[pl.ds(at, JOIN), :] = both
        nodes[pl.ds(LOW + at, JOIN), :] = pltpu.roll(both, ORB, 1)
        return carry

    turns = LOW // JOIN
    gets[0].wait()
    gets[1].wait()
    lax.fori_loop(0, turns // 2, join, 0)
    gets[2].wait()
    gets[3].wait()
    lax.fori_loop(turns // 2, turns, join, 0)
    gets[4].wait()
    come = jnp.where(inner, edge[...].astype(F32), 0.0)
    ghosts[:HALF_GHOST, :] = come
    ghosts[HALF_GHOST:, :] = pltpu.roll(come, ORB, 1)
    count = GHOST // PICK_TURNS

    def add(t, carry):
        for p in range(0, count, PICKS):
            at = t * count + p
            to = [bound_ref[at + j] for j in range(PICKS)]
            base = pl.multiple_of(at, 16)
            sums = [nodes[pl.ds(i, 1), :] + ghosts[pl.ds(base + j, 1), :] for j, i in enumerate(to)]
            for i, value in zip(to, sums):
                nodes[pl.ds(i, 1), :] = value
        return carry

    lax.fori_loop(0, PICK_TURNS, add, 0)
    for copy in parts:
        copy.wait()

    def turn(b, carry):
        at = pl.multiple_of(b * TURN, 128)
        rounded = nodes[pl.ds(at, TURN), :].astype(BF16)
        term_ref[...] += jnp.dot(panels[:, pl.ds(at, TURN)], rounded, preferred_element_type=F32)
        turned[:, pl.ds(at, TURN)] = rounded.T[:ORB, :]
        return carry

    lax.fori_loop(0, OWN // TURN, turn, 0)
    whole = pltpu.make_async_copy(turned, applied_ref, sems.at[9])
    whole.start()
    whole.wait()


def finish(boundary, own, got, edge, panels, far, side):
    return pl.pallas_call(
        finish_kernel,
        out_shape=(jax.ShapeDtypeStruct((ORB, OWN), BF16), jax.ShapeDtypeStruct((PANELS, 128), F32)),
        in_specs=[SMEM, ANY, ANY, ANY, ANY, ANY, ANY],
        out_specs=(ANY, VMEM),
        scratch_shapes=[
            pltpu.VMEM((LOW, 128), F32),
            pltpu.VMEM((LOW, 128), BF16),
            pltpu.VMEM((HALF_GHOST, 128), BF16),
            pltpu.VMEM((PANELS, OWN), BF16),
            pltpu.VMEM((2 * LOW, 128), F32),
            pltpu.VMEM((GHOST, 128), F32),
            pltpu.VMEM((ORB, OWN), BF16),
            pltpu.SemaphoreType.DMA((10,)),
        ],
        compiler_params=pltpu.CompilerParams(vmem_limit_bytes=VMEM_LIMIT),
    )(boundary, own, got, edge, panels, far, side)


def total_kernel(term_ref, out_ref, far, mid, near, held_mid, held_near, ss, sr):
    cell = lax.axis_index("cell")
    z, y, x = cell // 16, lax.rem(cell // 4, 4), lax.rem(cell, 4)

    def at(axis, d):
        place = [z, y, x]
        place[axis] = lax.rem(place[axis] + d, 4)
        return place[axis], {"cell": place[0] * 16 + place[1] * 4 + place[2]}

    greet([at(axis, d)[1] for axis in range(3) for d in range(1, 4)], 9)

    def exchange(axis, source, landing):
        copies = []
        for d in range(1, 4):
            to, device = at(axis, d)
            copies.append(remote(source.at[to], landing.at[d - 1], ss.at[axis, d - 1], sr.at[axis, d - 1], device))
            copies[-1].start()
        for copy in copies:
            copy.wait_recv()
        return copies

    started = exchange(0, term_ref, far)
    some = term_ref[z] + (far[0] + far[1] + far[2])
    for q in range(4):
        held_mid[q] = some[8 * q : 8 * q + 8]
    started += exchange(1, held_mid, mid)
    few = held_mid[y] + (mid[0] + mid[1] + mid[2])
    for q in range(4):
        held_near[q] = few[2 * q : 2 * q + 2]
    started += exchange(2, held_near, near)
    out_ref[...] = (held_near[x] + (near[0] + near[1] + near[2]))[:, :ORB]
    for copy in started:
        copy.wait_send()


def total(terms):
    return pl.pallas_call(
        total_kernel,
        out_shape=jax.ShapeDtypeStruct((2, ORB), F32),
        in_specs=[VMEM],
        out_specs=VMEM,
        scratch_shapes=[
            pltpu.VMEM((3, 32, 128), F32),
            pltpu.VMEM((3, 8, 128), F32),
            pltpu.VMEM((3, 2, 128), F32),
            pltpu.VMEM((4, 8, 128), F32),
            pltpu.VMEM((4, 2, 128), F32),
            pltpu.SemaphoreType.DMA((3, 3)),
            pltpu.SemaphoreType.DMA((3, 3)),
        ],
        compiler_params=pltpu.CompilerParams(collective_id=2, has_side_effects=True, vmem_limit_bytes=VMEM_LIMIT),
    )(terms)


def shards(orbitals, panels, stiffness, potential, connectivity, boundary):
    table = collect(orbitals, boundary)
    panels, table = lax.optimization_barrier((panels, table))
    far = lax.ppermute(panels, "orb", [(0, 2), (2, 0), (1, 3), (3, 1)])
    own, leave = elements(connectivity, potential, stiffness, table)
    got, edge, side = swap(own, leave, panels, far)
    applied, term = finish(boundary, own, got, edge, panels, far, side)
    return applied, total(term.reshape(4, PANELS // 4, 128))


def solution(mesh):
    return jax.shard_map(
        shards,
        mesh=mesh,
        in_specs=(
            P("orb", "cell"),
            P("orb", "cell"),
            P(),
            P(None, "cell"),
            P(None, "cell"),
            P("cell"),
        ),
        out_specs=(P("orb", "cell"), P("cell", "orb")),
        check_vma=False,
    )
```

```python
import jax
import jax.numpy as jnp
from jax import lax
from jax.experimental import pallas as pl
from jax.experimental.pallas import tpu as pltpu
from jax.sharding import PartitionSpec as P

ORB = 64
NPE = 343
ROWS = 344
DEEP = 384
CELLS = 48
HALF_CELLS = 24
OWN = 10368
GHOST = 1728
LOCAL = OWN + GHOST
PANELS = 128
N_CELL = 64
LOW = 5248
HALF_GHOST = 864
PACKED = LOW + HALF_GHOST
BATCH = 8
VMEM_LIMIT = 63 * 2**20
NODE_PACK = 656
GHOST_PACK = 432
TEAM = 4
ANY = pl.BlockSpec(memory_space=pltpu.HBM)
VMEM = pl.BlockSpec(memory_space=pltpu.VMEM)
SMEM = pl.BlockSpec(memory_space=pltpu.SMEM)
MESH = pl.DeviceIdType.MESH
F32 = jnp.float32
BF16 = jnp.bfloat16


def places():
    cell = lax.axis_index("cell")
    orb = lax.axis_index("orb")
    core = lax.rem(orb, 2)
    peer = {"orb": orb + 1 - 2 * core}
    before = {"cell": lax.rem(cell + N_CELL - 1, N_CELL)}
    after = {"cell": lax.rem(cell + 1, N_CELL)}
    return cell, core, peer, before, after


def greet(signalled, waits):
    barrier = pltpu.get_barrier_semaphore()
    for device in signalled:
        pl.semaphore_signal(barrier, inc=1, device_id=device, device_id_type=MESH)
    pl.semaphore_wait(barrier, waits)


def remote(src, dst, send, recv, device):
    return pltpu.make_async_remote_copy(
        src_ref=src, dst_ref=dst, send_sem=send, recv_sem=recv, device_id=device, device_id_type=MESH
    )


X_CHUNKS = 3
X_WIDE = OWN // X_CHUNKS
X_TURN = 1152
G_CHUNKS = 3
G_ROWS = HALF_GHOST // G_CHUNKS
G_TURN = 48


def collect_kernel(
    orb_ref, bound_ref, out_ref, x, table, alone, low, high, leaving, landed, local_sem, xs_sem, xr_sem, gs_sem, gr_sem, fs_sem, fr_sem, out_sem
):
    cell, core, peer, before, after = places()
    inner = cell < N_CELL - 1
    sends = cell > 0
    mine = pl.ds(pl.multiple_of(core * ORB, ORB), ORB)
    columns = [pl.ds(c * X_WIDE, X_WIDE) for c in range(X_CHUNKS)]
    own = [pltpu.make_async_copy(orb_ref.at[:, s], x.at[mine, s], local_sem.at[c]) for c, s in enumerate(columns)]
    for copy in own:
        copy.start()
    barrier = pltpu.get_barrier_semaphore()
    pl.semaphore_signal(barrier, inc=1, device_id=peer, device_id_type=MESH)

    @pl.when(inner)
    def _():
        pl.semaphore_signal(barrier, inc=1, device_id=after, device_id_type=MESH)

    for c in range(X_CHUNKS):
        own[c].wait()

        def turn_own(b, carry, c=c):
            at = pl.multiple_of(c * X_WIDE + b * X_TURN, 128)
            alone[pl.ds(at, X_TURN), :ORB] = x[mine, pl.ds(at, X_TURN)].T.astype(F32)
            return carry

        lax.fori_loop(0, X_WIDE // X_TURN, turn_own, 0)

    lane = lax.broadcasted_iota(jnp.int32, (G_TURN, 2 * ORB), 1)
    sent, passed, given = [], [], []
    for g in range(G_CHUNKS):

        def pick(t, carry, g=g):
            at = g * G_ROWS + t * G_TURN
            for j in range(G_TURN):
                low[pl.ds(j, 1), :] = alone[pl.ds(bound_ref[at + j], 1), :]
                high[pl.ds(j, 1), :] = alone[pl.ds(bound_ref[HALF_GHOST + at + j], 1), :]
            both = jnp.where(lane < ORB, low[...], pltpu.roll(high[...], ORB, 1))
            leaving[pl.ds(pl.multiple_of(at, 16), G_TURN), :] = both.astype(BF16)
            return carry

        part = pl.ds(g * G_ROWS, G_ROWS)
        sent.append(remote(leaving.at[part], landed.at[core, part], gs_sem.at[g], gr_sem.at[g], before))
        passed.append(remote(landed.at[core, part], landed.at[core, part], fs_sem.at[g], fr_sem.at[g], peer))

        @pl.when(sends)
        def _(pick=pick):
            lax.fori_loop(0, G_ROWS // G_TURN, pick, 0)

        if g == 0:
            pl.semaphore_wait(barrier, jnp.where(sends, 2, 1))

        @pl.when(sends)
        def _(g=g):
            sent[g].start()

        given.append(remote(orb_ref.at[:, columns[g]], x.at[mine, columns[g]], xs_sem.at[g], xr_sem.at[g], peer))
        given[g].start()
    stored = []
    for c in range(X_CHUNKS):
        given[c].wait_recv()

        def turn(b, carry, c=c):
            at = pl.multiple_of(c * X_WIDE + b * X_TURN, 128)
            table[pl.ds(at, X_TURN), :] = x[:, pl.ds(at, X_TURN)].T.astype(F32)
            return carry

        lax.fori_loop(0, X_WIDE // X_TURN, turn, 0)
        part = pl.ds(c * X_WIDE, X_WIDE)
        stored.append(pltpu.make_async_copy(table.at[part], out_ref.at[part], out_sem.at[c]))
        stored[-1].start()
    part = pl.ds(OWN, GHOST)
    stored.append(pltpu.make_async_copy(table.at[part], out_ref.at[part], out_sem.at[X_CHUNKS]))

    @pl.when(inner)
    def _():
        for g in range(G_CHUNKS):
            sent[g].wait_recv()
            passed[g].start()
        for g in range(G_CHUNKS):
            passed[g].wait_recv()
            rows = pl.ds(g * G_ROWS, G_ROWS)
            zero, one = landed[0, rows, :].astype(F32), landed[1, rows, :].astype(F32)
            first = lax.broadcasted_iota(jnp.int32, (G_ROWS, 2 * ORB), 1) < ORB
            table[pl.ds(OWN + g * G_ROWS, G_ROWS), :] = jnp.where(first, zero, pltpu.roll(one, ORB, 1))
            table[pl.ds(OWN + HALF_GHOST + g * G_ROWS, G_ROWS), :] = jnp.where(first, pltpu.roll(zero, ORB, 1), one)
        for copy in passed:
            copy.wait_send()

    @pl.when(jnp.logical_not(inner))
    def _():
        table[OWN:, :] = jnp.zeros((GHOST, 2 * ORB), F32)

    stored[-1].start()
    for copy in given:
        copy.wait_send()

    @pl.when(sends)
    def _():
        for copy in sent:
            copy.wait_send()

    for copy in stored:
        copy.wait()


def collect(orbitals, boundary):
    dma = pltpu.SemaphoreType.DMA
    return pl.pallas_call(
        collect_kernel,
        out_shape=jax.ShapeDtypeStruct((LOCAL, 2 * ORB), F32),
        in_specs=[ANY, SMEM],
        out_specs=ANY,
        scratch_shapes=[
            pltpu.VMEM((2 * ORB, OWN), BF16),
            pltpu.VMEM((LOCAL, 2 * ORB), F32),
            pltpu.VMEM((OWN, 2 * ORB), F32),
            pltpu.VMEM((G_TURN, 2 * ORB), F32),
            pltpu.VMEM((G_TURN, 2 * ORB), F32),
            pltpu.VMEM((HALF_GHOST, 2 * ORB), BF16),
            pltpu.VMEM((2, HALF_GHOST, 2 * ORB), BF16),
            dma((X_CHUNKS,)),
            dma((X_CHUNKS,)),
            dma((X_CHUNKS,)),
            dma((G_CHUNKS,)),
            dma((G_CHUNKS,)),
            dma((G_CHUNKS,)),
            dma((G_CHUNKS,)),
            dma((X_CHUNKS + 1,)),
        ],
        compiler_params=pltpu.CompilerParams(collective_id=0, has_side_effects=True, vmem_limit_bytes=VMEM_LIMIT),
    )(orbitals, boundary)


def element_kernel(conn_hbm, conn_vec, pot_ref, stiff_ref, table_ref, own_ref, leave_ref, table, leaving, even, odd, near, early, weights, scaled, scaled_t, sems, conn_ref, list_sem):
    fetch = pltpu.make_async_copy(table_ref, table, sems.at[6])
    fetch.start()
    list_copy = pltpu.make_async_copy(conn_hbm, conn_ref, list_sem)
    list_copy.start()
    core = lax.rem(lax.axis_index("orb"), 2)
    first = core * HALF_CELLS
    even[...] = jnp.zeros_like(even)
    odd[...] = jnp.zeros_like(odd)
    near[:, NPE:, :] = jnp.zeros((TEAM, DEEP - NPE, 128), F32)
    weights[...] = jnp.zeros_like(weights)
    weights[:NPE, :NPE] = stiff_ref[...]
    scaled[...] = jnp.zeros_like(scaled)
    scaled[:CELLS, :NPE] = pot_ref[...]
    levels = scaled[...].T
    scaled_t[...] = levels

    alike = jnp.zeros((CELLS, 1), jnp.int32)
    for d in range(1, BATCH):
        same = conn_vec[:, : NPE - d] == conn_vec[:, d:NPE]
        alike = jnp.maximum(alike, jnp.max(same.astype(jnp.int32), axis=1, keepdims=True))
    repeats = jnp.max(alike)
    fetch.wait()
    list_copy.wait()

    def index(t, j):
        return conn_ref[(first + t) * NPE + j]

    def gather(t, js, team=range(TEAM)):
        for h in team:
            for j in js:
                near[h, pl.ds(j, 1), :] = table[pl.ds(index(t + h, j), 1), :]

    def multiply(t):
        full = jnp.concatenate([near[h] for h in range(TEAM)], axis=1).astype(BF16)
        out = jnp.dot(weights[...], full, preferred_element_type=F32)
        for h in range(TEAM):
            level = jnp.take_along_axis(scaled_t[:ROWS, :], jnp.full((ROWS, 128), first + t + h, jnp.int32), axis=1)
            early[h] = out[:, h * 128 : h * 128 + 128] + level * near[h, :ROWS, :]

    def scatter(t, js, team=range(TEAM)):
        for h in team:
            total = odd if h % 2 else even
            at = [index(t + h, j) for j in js]
            sums = [total[pl.ds(i, 1), :] + early[h, pl.ds(j, 1), :] for i, j in zip(at, js)]
            for i, value in zip(at, sums):
                total[pl.ds(i, 1), :] = value

    batches = [range(b, min(NPE, b + BATCH)) for b in range(0, NPE, BATCH)]

    def team(u, carry):
        t = TEAM * u
        for js in batches:
            for h in range(TEAM):
                gather(t, js, [h])
                scatter(jnp.maximum(t - TEAM, 0), js, [h])

        @pl.when(t >= 0)
        def _():
            multiply(t)

        return carry

    @pl.when(repeats == 0)
    def _():
        early[...] = jnp.zeros_like(early)
        lax.fori_loop(0, HALF_CELLS // TEAM, team, 0)
        for js in batches:
            scatter(HALF_CELLS - TEAM, js)

    @pl.when(repeats != 0)
    def _():
        def one(u, carry):
            def pick(j, inner):
                gather(TEAM * u, [j])
                return inner

            def add(j, inner):
                for h in range(TEAM):
                    i = index(TEAM * u + h, j)
                    even[pl.ds(i, 1), :] = even[pl.ds(i, 1), :] + early[h, pl.ds(j, 1), :]
                return inner

            lax.fori_loop(0, NPE, pick, 0)
            multiply(TEAM * u)
            lax.fori_loop(0, NPE, add, 0)
            return carry

        lax.fori_loop(0, HALF_CELLS // TEAM, one, 0)

    puts = []

    def pack(low, high, to, count):
        lane = lax.broadcasted_iota(jnp.int32, (count, 128), 1)
        straight = (lane < ORB) == (core == 0)
        low, high, to = (pl.ds(s, count) for s in (low, high, to))
        a = even[low, :] + odd[low, :]
        b = even[high, :] + odd[high, :]
        kept = jnp.where(lane < ORB, a, b)
        moved = pltpu.roll(jnp.where(lane < ORB, b, a), ORB, 1)
        table[to, :] = jnp.where(straight, kept, moved)
        leaving[to, :] = jnp.where(straight, moved, kept).astype(BF16)

    def put(start, count):
        part = pl.ds(start, count)
        puts.append(pltpu.make_async_copy(table.at[part], own_ref.at[part], sems.at[len(puts)]))
        puts[-1].start()
        puts.append(pltpu.make_async_copy(leaving.at[part], leave_ref.at[part], sems.at[len(puts)]))
        puts[-1].start()

    def pack_ghosts(r, carry):
        at = pl.multiple_of(r * GHOST_PACK, 16)
        pack(OWN + at, OWN + HALF_GHOST + at, LOW + at, GHOST_PACK)
        return carry

    def pack_nodes(r, carry):
        at = pl.multiple_of(r * NODE_PACK, 16)
        pack(at, LOW + at, at, NODE_PACK)
        return carry

    lax.fori_loop(0, HALF_GHOST // GHOST_PACK, pack_ghosts, 0)
    put(LOW, HALF_GHOST)
    turns = LOW // NODE_PACK
    lax.fori_loop(0, turns // 2, pack_nodes, 0)
    put(0, LOW // 2)
    lax.fori_loop(turns // 2, turns, pack_nodes, 0)
    put(LOW // 2, LOW // 2)
    for copy in puts:
        copy.wait()


def elements(connectivity, potential, stiffness, table):
    return pl.pallas_call(
        element_kernel,
        out_shape=(jax.ShapeDtypeStruct((PACKED, 128), F32), jax.ShapeDtypeStruct((PACKED, 128), BF16)),
        in_specs=[ANY, VMEM, VMEM, VMEM, ANY],
        out_specs=(ANY, ANY),
        scratch_shapes=[
            pltpu.VMEM((LOCAL, 128), F32),
            pltpu.VMEM((PACKED, 128), BF16),
            pltpu.VMEM((LOCAL, 128), F32),
            pltpu.VMEM((LOCAL, 128), F32),
            pltpu.VMEM((TEAM, DEEP, 128), F32),
            pltpu.VMEM((TEAM, ROWS, 128), F32),
            pltpu.VMEM((ROWS, DEEP), BF16),
            pltpu.VMEM((128, DEEP), F32),
            pltpu.VMEM((DEEP, 128), F32),
            pltpu.SemaphoreType.DMA((7,)),
            pltpu.SMEM((CELLS * NPE,), jnp.int32),
            pltpu.SemaphoreType.DMA,
        ],
        compiler_params=pltpu.CompilerParams(vmem_limit_bytes=VMEM_LIMIT),
        cost_estimate=pl.CostEstimate(flops=2 * HALF_CELLS * NPE * NPE * 128, bytes_accessed=60 * 2**20, transcendentals=0),
    )(connectivity.T.reshape(-1), connectivity.T, potential.T, stiffness, table)


def swap_kernel(own_ref, leave_ref, panels_ref, far_ref, got_ref, in_ref, side_ref, edge, other, leaving, sem, ss, sr, gs, gr, es, er):
    cell, core, peer, before, after = places()
    mine = pltpu.make_async_copy(own_ref.at[pl.ds(LOW, HALF_GHOST)], edge, sem)
    mine.start()
    inner = cell > 0
    sends = cell < N_CELL - 1
    barrier = pltpu.get_barrier_semaphore()
    pl.semaphore_signal(barrier, inc=1, device_id=peer, device_id_type=MESH)

    @pl.when(inner)
    def _():
        pl.semaphore_signal(barrier, inc=1, device_id=before, device_id_type=MESH)

    pl.semaphore_wait(barrier, jnp.where(sends, 2, 1))
    ghosts, shared = [], []
    for g in range(G_CHUNKS):
        part = pl.ds(g * G_ROWS, G_ROWS)
        ghosts.append(remote(leave_ref.at[pl.ds(LOW + g * G_ROWS, G_ROWS)], other.at[part], gs.at[g], gr.at[g], peer))
        ghosts[-1].start()
        shared.append(remote(leaving.at[part], in_ref.at[part], es.at[g], er.at[g], after))
    nodes = remote(leave_ref.at[pl.ds(0, LOW)], got_ref, ss.at[0], sr.at[0], peer)
    nodes.start()
    rows = panels_ref.shape[0]
    near = remote(panels_ref, side_ref.at[pl.ds(0, rows)], ss.at[1], sr.at[1], peer)
    near.start()
    far = remote(far_ref, side_ref.at[pl.ds(rows, rows)], ss.at[2], sr.at[2], peer)
    far.start()
    mine.wait()
    for g in range(G_CHUNKS):
        ghosts[g].wait_recv()
        part = pl.ds(g * G_ROWS, G_ROWS)

        @pl.when(sends)
        def _(g=g, part=part):
            leaving[part, :] = (edge[part, :] + other[part, :].astype(F32)).astype(BF16)
            shared[g].start()

    for copy in (nodes, near, far):
        copy.wait_recv()

    @pl.when(inner)
    def _():
        for copy in shared:
            copy.wait_recv()

    for copy in [*ghosts, nodes, near, far]:
        copy.wait_send()

    @pl.when(sends)
    def _():
        for copy in shared:
            copy.wait_send()


def swap(own, leave, panels, far):
    rows = panels.shape[0]
    return pl.pallas_call(
        swap_kernel,
        out_shape=(
            jax.ShapeDtypeStruct((LOW, 128), BF16),
            jax.ShapeDtypeStruct((HALF_GHOST, 128), BF16),
            jax.ShapeDtypeStruct((2 * rows, OWN), BF16),
        ),
        in_specs=[ANY, ANY, ANY, ANY],
        out_specs=(ANY, ANY, ANY),
        scratch_shapes=[
            pltpu.VMEM((HALF_GHOST, 128), F32),
            pltpu.VMEM((HALF_GHOST, 128), BF16),
            pltpu.VMEM((HALF_GHOST, 128), BF16),
            pltpu.SemaphoreType.DMA,
            pltpu.SemaphoreType.DMA((3,)),
            pltpu.SemaphoreType.DMA((3,)),
            pltpu.SemaphoreType.DMA((G_CHUNKS,)),
            pltpu.SemaphoreType.DMA((G_CHUNKS,)),
            pltpu.SemaphoreType.DMA((G_CHUNKS,)),
            pltpu.SemaphoreType.DMA((G_CHUNKS,)),
        ],
        compiler_params=pltpu.CompilerParams(collective_id=1, has_side_effects=True, vmem_limit_bytes=VMEM_LIMIT),
    )(own, leave, panels, far)


JOIN = 656
TURN = 1152
PICKS = 16
PICK_TURNS = 9


def finish_kernel(
    bound_ref, own_ref, got_ref, in_ref, mine_ref, far_ref, side_ref, applied_ref, term_ref, own, got, edge, panels, nodes, ghosts, turned, sems
):
    inner = lax.axis_index("cell") > 0
    gets = []
    for h in range(2):
        part = pl.ds(h * LOW // 2, LOW // 2)
        gets.append(pltpu.make_async_copy(own_ref.at[part], own.at[part], sems.at[2 * h]))
        gets.append(pltpu.make_async_copy(got_ref.at[part], got.at[part], sems.at[2 * h + 1]))
    gets.append(pltpu.make_async_copy(in_ref, edge, sems.at[4]))
    for copy in gets:
        copy.start()
    orb = lax.axis_index("orb")
    other, across = orb + 1 - 2 * lax.rem(orb, 2), lax.rem(orb + 2, 4)
    count = mine_ref.shape[0]
    sources = (mine_ref, far_ref, side_ref.at[pl.ds(0, count)], side_ref.at[pl.ds(count, count)])
    rows = (orb, across, other, lax.rem(other + 2, 4))
    parts = []
    for k, (source, row) in enumerate(zip(sources, rows)):
        to = panels.at[pl.ds(pl.multiple_of(row * count, count), count)]
        parts.append(pltpu.make_async_copy(source, to, sems.at[5 + k]))
        parts[-1].start()
    term_ref[...] = jnp.zeros_like(term_ref)

    def join(r, carry):
        at = pl.multiple_of(r * JOIN, 16)
        both = own[pl.ds(at, JOIN), :] + got[pl.ds(at, JOIN), :].astype(F32)
        nodes[pl.ds(at, JOIN), :] = both
        nodes[pl.ds(LOW + at, JOIN), :] = pltpu.roll(both, ORB, 1)
        return carry

    turns = LOW // JOIN
    gets[0].wait()
    gets[1].wait()
    lax.fori_loop(0, turns // 2, join, 0)
    gets[2].wait()
    gets[3].wait()
    lax.fori_loop(turns // 2, turns, join, 0)
    gets[4].wait()
    come = jnp.where(inner, edge[...].astype(F32), 0.0)
    ghosts[:HALF_GHOST, :] = come
    ghosts[HALF_GHOST:, :] = pltpu.roll(come, ORB, 1)
    count = GHOST // PICK_TURNS

    def add(t, carry):
        for p in range(0, count, PICKS):
            at = t * count + p
            to = [bound_ref[at + j] for j in range(PICKS)]
            base = pl.multiple_of(at, 16)
            sums = [nodes[pl.ds(i, 1), :] + ghosts[pl.ds(base + j, 1), :] for j, i in enumerate(to)]
            for i, value in zip(to, sums):
                nodes[pl.ds(i, 1), :] = value
        return carry

    lax.fori_loop(0, PICK_TURNS, add, 0)
    for copy in parts:
        copy.wait()

    puts = []
    for b in range(OWN // TURN):
        part = pl.ds(b * TURN, TURN)
        rounded = nodes[part, :].astype(BF16)
        term_ref[...] += jnp.dot(panels[:, part], rounded, preferred_element_type=F32)
        turned[:, part] = rounded.T[:ORB, :]
        puts.append(pltpu.make_async_copy(turned.at[:, part], applied_ref.at[:, part], sems.at[9 + b]))
        puts[-1].start()
    for copy in puts:
        copy.wait()


def finish(boundary, own, got, edge, panels, far, side):
    return pl.pallas_call(
        finish_kernel,
        out_shape=(jax.ShapeDtypeStruct((ORB, OWN), BF16), jax.ShapeDtypeStruct((PANELS, 128), F32)),
        in_specs=[SMEM, ANY, ANY, ANY, ANY, ANY, ANY],
        out_specs=(ANY, VMEM),
        scratch_shapes=[
            pltpu.VMEM((LOW, 128), F32),
            pltpu.VMEM((LOW, 128), BF16),
            pltpu.VMEM((HALF_GHOST, 128), BF16),
            pltpu.VMEM((PANELS, OWN), BF16),
            pltpu.VMEM((2 * LOW, 128), F32),
            pltpu.VMEM((GHOST, 128), F32),
            pltpu.VMEM((ORB, OWN), BF16),
            pltpu.SemaphoreType.DMA((9 + OWN // TURN,)),
        ],
        compiler_params=pltpu.CompilerParams(vmem_limit_bytes=VMEM_LIMIT),
    )(boundary, own, got, edge, panels, far, side)


def total_kernel(term_ref, out_ref, far, mid, near, held_mid, held_near, ss, sr):
    cell = lax.axis_index("cell")
    z, y, x = cell // 16, lax.rem(cell // 4, 4), lax.rem(cell, 4)

    def at(axis, d):
        place = [z, y, x]
        place[axis] = lax.rem(place[axis] + d, 4)
        return place[axis], {"cell": place[0] * 16 + place[1] * 4 + place[2]}

    greet([at(axis, d)[1] for axis in range(3) for d in range(1, 4)], 9)

    def exchange(axis, source, landing):
        copies = []
        for d in range(1, 4):
            to, device = at(axis, d)
            copies.append(remote(source.at[to], landing.at[d - 1], ss.at[axis, d - 1], sr.at[axis, d - 1], device))
            copies[-1].start()
        for copy in copies:
            copy.wait_recv()
        return copies

    started = exchange(0, term_ref, far)
    some = term_ref[z] + (far[0] + far[1] + far[2])
    for q in range(4):
        held_mid[q] = some[8 * q : 8 * q + 8]
    started += exchange(1, held_mid, mid)
    few = held_mid[y] + (mid[0] + mid[1] + mid[2])
    for q in range(4):
        held_near[q] = few[2 * q : 2 * q + 2]
    started += exchange(2, held_near, near)
    out_ref[...] = (held_near[x] + (near[0] + near[1] + near[2]))[:, :ORB]
    for copy in started:
        copy.wait_send()


def total(terms):
    return pl.pallas_call(
        total_kernel,
        out_shape=jax.ShapeDtypeStruct((2, ORB), F32),
        in_specs=[VMEM],
        out_specs=VMEM,
        scratch_shapes=[
            pltpu.VMEM((3, 32, 128), F32),
            pltpu.VMEM((3, 8, 128), F32),
            pltpu.VMEM((3, 2, 128), F32),
            pltpu.VMEM((4, 8, 128), F32),
            pltpu.VMEM((4, 2, 128), F32),
            pltpu.SemaphoreType.DMA((3, 3)),
            pltpu.SemaphoreType.DMA((3, 3)),
        ],
        compiler_params=pltpu.CompilerParams(collective_id=2, has_side_effects=True, vmem_limit_bytes=VMEM_LIMIT),
    )(terms)


def shards(orbitals, panels, stiffness, potential, connectivity, boundary):
    table = collect(orbitals, boundary)
    panels, table = lax.optimization_barrier((panels, table))
    far = lax.ppermute(panels, "orb", [(0, 2), (2, 0), (1, 3), (3, 1)])
    own, leave = elements(connectivity, potential, stiffness, table)
    got, edge, side = swap(own, leave, panels, far)
    applied, term = finish(boundary, own, got, edge, panels, far, side)
    return applied, total(term.reshape(4, PANELS // 4, 128))


def solution(mesh):
    return jax.shard_map(
        shards,
        mesh=mesh,
        in_specs=(
            P("orb", "cell"),
            P("orb", "cell"),
            P(),
            P(None, "cell"),
            P(None, "cell"),
            P("cell"),
        ),
        out_specs=(P("orb", "cell"), P("cell", "orb")),
        check_vma=False,
    )
```

```python
import jax
import jax.numpy as jnp
from jax import lax
from jax.experimental import pallas as pl
from jax.experimental.pallas import tpu as pltpu
from jax.sharding import PartitionSpec as P

ORB = 64
NPE = 343
ROWS = 344
DEEP = 384
CELLS = 48
HALF_CELLS = 24
OWN = 10368
GHOST = 1728
LOCAL = OWN + GHOST
PANELS = 128
N_CELL = 64
LOW = 5248
HALF_GHOST = 864
PACKED = LOW + HALF_GHOST
BATCH = 8
VMEM_LIMIT = 63 * 2**20
NODE_PACK = 656
GHOST_PACK = 432
TEAM = 4
ANY = pl.BlockSpec(memory_space=pltpu.HBM)
VMEM = pl.BlockSpec(memory_space=pltpu.VMEM)
SMEM = pl.BlockSpec(memory_space=pltpu.SMEM)
MESH = pl.DeviceIdType.MESH
F32 = jnp.float32
BF16 = jnp.bfloat16


def places():
    cell = lax.axis_index("cell")
    orb = lax.axis_index("orb")
    core = lax.rem(orb, 2)
    peer = {"orb": orb + 1 - 2 * core}
    before = {"cell": lax.rem(cell + N_CELL - 1, N_CELL)}
    after = {"cell": lax.rem(cell + 1, N_CELL)}
    return cell, core, peer, before, after


def greet(signalled, waits):
    barrier = pltpu.get_barrier_semaphore()
    for device in signalled:
        pl.semaphore_signal(barrier, inc=1, device_id=device, device_id_type=MESH)
    pl.semaphore_wait(barrier, waits)


def remote(src, dst, send, recv, device):
    return pltpu.make_async_remote_copy(
        src_ref=src, dst_ref=dst, send_sem=send, recv_sem=recv, device_id=device, device_id_type=MESH
    )


X_CHUNKS = 3
X_WIDE = OWN // X_CHUNKS
X_TURN = 1152
G_CHUNKS = 3
G_ROWS = HALF_GHOST // G_CHUNKS
G_TURN = 48


def collect_kernel(
    orb_ref, bound_ref, out_ref, x, table, alone, low, high, leaving, landed, local_sem, xs_sem, xr_sem, gs_sem, gr_sem, fs_sem, fr_sem, out_sem
):
    cell, core, peer, before, after = places()
    inner = cell < N_CELL - 1
    sends = cell > 0
    mine = pl.ds(pl.multiple_of(core * ORB, ORB), ORB)
    columns = [pl.ds(c * X_WIDE, X_WIDE) for c in range(X_CHUNKS)]
    own = [pltpu.make_async_copy(orb_ref.at[:, s], x.at[mine, s], local_sem.at[c]) for c, s in enumerate(columns)]
    for copy in own:
        copy.start()
    barrier = pltpu.get_barrier_semaphore()
    pl.semaphore_signal(barrier, inc=1, device_id=peer, device_id_type=MESH)

    @pl.when(inner)
    def _():
        pl.semaphore_signal(barrier, inc=1, device_id=after, device_id_type=MESH)

    for c in range(X_CHUNKS):
        own[c].wait()

        def turn_own(b, carry, c=c):
            at = pl.multiple_of(c * X_WIDE + b * X_TURN, 128)
            alone[pl.ds(at, X_TURN), :ORB] = x[mine, pl.ds(at, X_TURN)].T.astype(F32)
            return carry

        lax.fori_loop(0, X_WIDE // X_TURN, turn_own, 0)

    lane = lax.broadcasted_iota(jnp.int32, (G_TURN, 2 * ORB), 1)
    sent, passed, given = [], [], []
    for g in range(G_CHUNKS):

        def pick(t, carry, g=g):
            at = g * G_ROWS + t * G_TURN
            for j in range(G_TURN):
                low[pl.ds(j, 1), :] = alone[pl.ds(bound_ref[at + j], 1), :]
                high[pl.ds(j, 1), :] = alone[pl.ds(bound_ref[HALF_GHOST + at + j], 1), :]
            both = jnp.where(lane < ORB, low[...], pltpu.roll(high[...], ORB, 1))
            leaving[pl.ds(pl.multiple_of(at, 16), G_TURN), :] = both.astype(BF16)
            return carry

        part = pl.ds(g * G_ROWS, G_ROWS)
        sent.append(remote(leaving.at[part], landed.at[core, part], gs_sem.at[g], gr_sem.at[g], before))
        passed.append(remote(landed.at[core, part], landed.at[core, part], fs_sem.at[g], fr_sem.at[g], peer))

        @pl.when(sends)
        def _(pick=pick):
            lax.fori_loop(0, G_ROWS // G_TURN, pick, 0)

        if g == 0:
            pl.semaphore_wait(barrier, jnp.where(sends, 2, 1))

        @pl.when(sends)
        def _(g=g):
            sent[g].start()

        given.append(remote(orb_ref.at[:, columns[g]], x.at[mine, columns[g]], xs_sem.at[g], xr_sem.at[g], peer))
        given[g].start()
    stored = []
    for c in range(X_CHUNKS):
        given[c].wait_recv()

        def turn(b, carry, c=c):
            at = pl.multiple_of(c * X_WIDE + b * X_TURN, 128)
            table[pl.ds(at, X_TURN), :] = x[:, pl.ds(at, X_TURN)].T.astype(F32)
            return carry

        lax.fori_loop(0, X_WIDE // X_TURN, turn, 0)
        part = pl.ds(c * X_WIDE, X_WIDE)
        stored.append(pltpu.make_async_copy(table.at[part], out_ref.at[part], out_sem.at[c]))
        stored[-1].start()
    part = pl.ds(OWN, GHOST)
    stored.append(pltpu.make_async_copy(table.at[part], out_ref.at[part], out_sem.at[X_CHUNKS]))

    @pl.when(inner)
    def _():
        for g in range(G_CHUNKS):
            sent[g].wait_recv()
            passed[g].start()
        for g in range(G_CHUNKS):
            passed[g].wait_recv()
            rows = pl.ds(g * G_ROWS, G_ROWS)
            zero, one = landed[0, rows, :].astype(F32), landed[1, rows, :].astype(F32)
            first = lax.broadcasted_iota(jnp.int32, (G_ROWS, 2 * ORB), 1) < ORB
            table[pl.ds(OWN + g * G_ROWS, G_ROWS), :] = jnp.where(first, zero, pltpu.roll(one, ORB, 1))
            table[pl.ds(OWN + HALF_GHOST + g * G_ROWS, G_ROWS), :] = jnp.where(first, pltpu.roll(zero, ORB, 1), one)
        for copy in passed:
            copy.wait_send()

    @pl.when(jnp.logical_not(inner))
    def _():
        table[OWN:, :] = jnp.zeros((GHOST, 2 * ORB), F32)

    stored[-1].start()
    for copy in given:
        copy.wait_send()

    @pl.when(sends)
    def _():
        for copy in sent:
            copy.wait_send()

    for copy in stored:
        copy.wait()


def collect(orbitals, boundary):
    dma = pltpu.SemaphoreType.DMA
    return pl.pallas_call(
        collect_kernel,
        out_shape=jax.ShapeDtypeStruct((LOCAL, 2 * ORB), F32),
        in_specs=[ANY, SMEM],
        out_specs=ANY,
        scratch_shapes=[
            pltpu.VMEM((2 * ORB, OWN), BF16),
            pltpu.VMEM((LOCAL, 2 * ORB), F32),
            pltpu.VMEM((OWN, 2 * ORB), F32),
            pltpu.VMEM((G_TURN, 2 * ORB), F32),
            pltpu.VMEM((G_TURN, 2 * ORB), F32),
            pltpu.VMEM((HALF_GHOST, 2 * ORB), BF16),
            pltpu.VMEM((2, HALF_GHOST, 2 * ORB), BF16),
            dma((X_CHUNKS,)),
            dma((X_CHUNKS,)),
            dma((X_CHUNKS,)),
            dma((G_CHUNKS,)),
            dma((G_CHUNKS,)),
            dma((G_CHUNKS,)),
            dma((G_CHUNKS,)),
            dma((X_CHUNKS + 1,)),
        ],
        compiler_params=pltpu.CompilerParams(collective_id=0, has_side_effects=True, vmem_limit_bytes=VMEM_LIMIT),
    )(orbitals, boundary)


def element_kernel(conn_hbm, conn_vec, pot_ref, stiff_ref, table_ref, own_ref, leave_ref, table, leaving, even, odd, near, early, weights, scaled, scaled_t, sems, conn_ref, list_sem):
    fetch = pltpu.make_async_copy(table_ref, table, sems.at[6])
    fetch.start()
    list_copy = pltpu.make_async_copy(conn_hbm, conn_ref, list_sem)
    list_copy.start()
    core = lax.rem(lax.axis_index("orb"), 2)
    first = core * HALF_CELLS
    even[...] = jnp.zeros_like(even)
    odd[...] = jnp.zeros_like(odd)
    near[:, NPE:, :] = jnp.zeros((TEAM, DEEP - NPE, 128), F32)
    weights[...] = jnp.zeros_like(weights)
    weights[:NPE, :NPE] = stiff_ref[...]
    scaled[...] = jnp.zeros_like(scaled)
    scaled[:CELLS, :NPE] = pot_ref[...]
    levels = scaled[...].T
    scaled_t[...] = levels

    alike = jnp.zeros((CELLS, 1), jnp.int32)
    for d in range(1, BATCH):
        same = conn_vec[:, : NPE - d] == conn_vec[:, d:NPE]
        alike = jnp.maximum(alike, jnp.max(same.astype(jnp.int32), axis=1, keepdims=True))
    repeats = jnp.max(alike)
    fetch.wait()
    list_copy.wait()

    def index(t, j):
        return conn_ref[(first + t) * NPE + j]

    def gather(t, js, team=range(TEAM)):
        for h in team:
            for j in js:
                near[h, pl.ds(j, 1), :] = table[pl.ds(index(t + h, j), 1), :]

    def multiply(t):
        full = jnp.concatenate([near[h] for h in range(TEAM)], axis=1).astype(BF16)
        out = jnp.dot(weights[...], full, preferred_element_type=F32)
        for h in range(TEAM):
            level = jnp.take_along_axis(scaled_t[:ROWS, :], jnp.full((ROWS, 128), first + t + h, jnp.int32), axis=1)
            early[h] = out[:, h * 128 : h * 128 + 128] + level * near[h, :ROWS, :]

    def scatter(t, js, team=range(TEAM)):
        for h in team:
            total = odd if h % 2 else even
            at = [index(t + h, j) for j in js]
            sums = [total[pl.ds(i, 1), :] + early[h, pl.ds(j, 1), :] for i, j in zip(at, js)]
            for i, value in zip(at, sums):
                total[pl.ds(i, 1), :] = value

    batches = [range(b, min(NPE, b + BATCH)) for b in range(0, NPE, BATCH)]

    def team(u, carry):
        t = TEAM * u
        for js in batches:
            for h in range(TEAM):
                gather(t, js, [h])
                scatter(jnp.maximum(t - TEAM, 0), js, [h])

        @pl.when(t >= 0)
        def _():
            multiply(t)

        return carry

    @pl.when(repeats == 0)
    def _():
        early[...] = jnp.zeros_like(early)
        lax.fori_loop(0, HALF_CELLS // TEAM, team, 0)
        for js in batches:
            scatter(HALF_CELLS - TEAM, js)

    @pl.when(repeats != 0)
    def _():
        def one(u, carry):
            def pick(j, inner):
                gather(TEAM * u, [j])
                return inner

            def add(j, inner):
                for h in range(TEAM):
                    i = index(TEAM * u + h, j)
                    even[pl.ds(i, 1), :] = even[pl.ds(i, 1), :] + early[h, pl.ds(j, 1), :]
                return inner

            lax.fori_loop(0, NPE, pick, 0)
            multiply(TEAM * u)
            lax.fori_loop(0, NPE, add, 0)
            return carry

        lax.fori_loop(0, HALF_CELLS // TEAM, one, 0)

    puts = []

    def pack(low, high, to, count):
        lane = lax.broadcasted_iota(jnp.int32, (count, 128), 1)
        straight = (lane < ORB) == (core == 0)
        low, high, to = (pl.ds(s, count) for s in (low, high, to))
        a = even[low, :] + odd[low, :]
        b = even[high, :] + odd[high, :]
        kept = jnp.where(lane < ORB, a, b)
        moved = pltpu.roll(jnp.where(lane < ORB, b, a), ORB, 1)
        table[to, :] = jnp.where(straight, kept, moved)
        leaving[to, :] = jnp.where(straight, moved, kept).astype(BF16)

    def put(start, count):
        part = pl.ds(start, count)
        puts.append(pltpu.make_async_copy(table.at[part], own_ref.at[part], sems.at[len(puts)]))
        puts[-1].start()
        puts.append(pltpu.make_async_copy(leaving.at[part], leave_ref.at[part], sems.at[len(puts)]))
        puts[-1].start()

    def pack_ghosts(r, carry):
        at = pl.multiple_of(r * GHOST_PACK, 16)
        pack(OWN + at, OWN + HALF_GHOST + at, LOW + at, GHOST_PACK)
        return carry

    def pack_nodes(r, carry):
        at = pl.multiple_of(r * NODE_PACK, 16)
        pack(at, LOW + at, at, NODE_PACK)
        return carry

    lax.fori_loop(0, HALF_GHOST // GHOST_PACK, pack_ghosts, 0)
    put(LOW, HALF_GHOST)
    turns = LOW // NODE_PACK
    lax.fori_loop(0, turns // 2, pack_nodes, 0)
    put(0, LOW // 2)
    lax.fori_loop(turns // 2, turns, pack_nodes, 0)
    put(LOW // 2, LOW // 2)
    for copy in puts:
        copy.wait()


def elements(connectivity, potential, stiffness, table):
    return pl.pallas_call(
        element_kernel,
        out_shape=(jax.ShapeDtypeStruct((PACKED, 128), F32), jax.ShapeDtypeStruct((PACKED, 128), BF16)),
        in_specs=[ANY, VMEM, VMEM, VMEM, ANY],
        out_specs=(ANY, ANY),
        scratch_shapes=[
            pltpu.VMEM((LOCAL, 128), F32),
            pltpu.VMEM((PACKED, 128), BF16),
            pltpu.VMEM((LOCAL, 128), F32),
            pltpu.VMEM((LOCAL, 128), F32),
            pltpu.VMEM((TEAM, DEEP, 128), F32),
            pltpu.VMEM((TEAM, ROWS, 128), F32),
            pltpu.VMEM((ROWS, DEEP), BF16),
            pltpu.VMEM((128, DEEP), F32),
            pltpu.VMEM((DEEP, 128), F32),
            pltpu.SemaphoreType.DMA((7,)),
            pltpu.SMEM((CELLS * NPE,), jnp.int32),
            pltpu.SemaphoreType.DMA,
        ],
        compiler_params=pltpu.CompilerParams(vmem_limit_bytes=VMEM_LIMIT),
        cost_estimate=pl.CostEstimate(flops=2 * HALF_CELLS * NPE * NPE * 128, bytes_accessed=60 * 2**20, transcendentals=0),
    )(connectivity.T.reshape(-1), connectivity.T, potential.T, stiffness, table)


def swap_kernel(own_ref, leave_ref, panels_ref, far_ref, got_ref, in_ref, side_ref, edge, other, leaving, sem, ss, sr, gs, gr, es, er):
    cell, core, peer, before, after = places()
    mine = pltpu.make_async_copy(own_ref.at[pl.ds(LOW, HALF_GHOST)], edge, sem)
    mine.start()
    inner = cell > 0
    sends = cell < N_CELL - 1
    barrier = pltpu.get_barrier_semaphore()
    pl.semaphore_signal(barrier, inc=1, device_id=peer, device_id_type=MESH)

    @pl.when(inner)
    def _():
        pl.semaphore_signal(barrier, inc=1, device_id=before, device_id_type=MESH)

    pl.semaphore_wait(barrier, jnp.where(sends, 2, 1))
    ghosts, shared = [], []
    for g in range(G_CHUNKS):
        part = pl.ds(g * G_ROWS, G_ROWS)
        ghosts.append(remote(leave_ref.at[pl.ds(LOW + g * G_ROWS, G_ROWS)], other.at[part], gs.at[g], gr.at[g], peer))
        ghosts[-1].start()
        shared.append(remote(leaving.at[part], in_ref.at[part], es.at[g], er.at[g], after))
    nodes = remote(leave_ref.at[pl.ds(0, LOW)], got_ref, ss.at[0], sr.at[0], peer)
    nodes.start()
    rows = panels_ref.shape[0]
    near = remote(panels_ref, side_ref.at[pl.ds(0, rows)], ss.at[1], sr.at[1], peer)
    near.start()
    far = remote(far_ref, side_ref.at[pl.ds(rows, rows)], ss.at[2], sr.at[2], peer)
    far.start()
    mine.wait()
    for g in range(G_CHUNKS):
        ghosts[g].wait_recv()
        part = pl.ds(g * G_ROWS, G_ROWS)

        @pl.when(sends)
        def _(g=g, part=part):
            leaving[part, :] = (edge[part, :] + other[part, :].astype(F32)).astype(BF16)
            shared[g].start()

    for copy in (nodes, near, far):
        copy.wait_recv()

    @pl.when(inner)
    def _():
        for copy in shared:
            copy.wait_recv()

    for copy in [*ghosts, nodes, near, far]:
        copy.wait_send()

    @pl.when(sends)
    def _():
        for copy in shared:
            copy.wait_send()


def swap(own, leave, panels, far):
    rows = panels.shape[0]
    return pl.pallas_call(
        swap_kernel,
        out_shape=(
            jax.ShapeDtypeStruct((LOW, 128), BF16),
            jax.ShapeDtypeStruct((HALF_GHOST, 128), BF16),
            jax.ShapeDtypeStruct((2 * rows, OWN), BF16),
        ),
        in_specs=[ANY, ANY, ANY, ANY],
        out_specs=(ANY, ANY, ANY),
        scratch_shapes=[
            pltpu.VMEM((HALF_GHOST, 128), F32),
            pltpu.VMEM((HALF_GHOST, 128), BF16),
            pltpu.VMEM((HALF_GHOST, 128), BF16),
            pltpu.SemaphoreType.DMA,
            pltpu.SemaphoreType.DMA((3,)),
            pltpu.SemaphoreType.DMA((3,)),
            pltpu.SemaphoreType.DMA((G_CHUNKS,)),
            pltpu.SemaphoreType.DMA((G_CHUNKS,)),
            pltpu.SemaphoreType.DMA((G_CHUNKS,)),
            pltpu.SemaphoreType.DMA((G_CHUNKS,)),
        ],
        compiler_params=pltpu.CompilerParams(collective_id=1, has_side_effects=True, vmem_limit_bytes=VMEM_LIMIT),
    )(own, leave, panels, far)


JOIN = 656
TURN = 1152
PICKS = 16
PICK_TURNS = 9


def finish_kernel(
    bound_ref, own_ref, got_ref, in_ref, mine_ref, far_ref, side_ref, applied_ref, term_ref, own, got, edge, panels, nodes, ghosts, turned, sems
):
    inner = lax.axis_index("cell") > 0
    gets = []
    for h in range(2):
        part = pl.ds(h * LOW // 2, LOW // 2)
        gets.append(pltpu.make_async_copy(own_ref.at[part], own.at[part], sems.at[2 * h]))
        gets.append(pltpu.make_async_copy(got_ref.at[part], got.at[part], sems.at[2 * h + 1]))
    gets.append(pltpu.make_async_copy(in_ref, edge, sems.at[4]))
    for copy in gets:
        copy.start()
    orb = lax.axis_index("orb")
    other, across = orb + 1 - 2 * lax.rem(orb, 2), lax.rem(orb + 2, 4)
    count = mine_ref.shape[0]
    sources = (mine_ref, far_ref, side_ref.at[pl.ds(0, count)], side_ref.at[pl.ds(count, count)])
    rows = (orb, across, other, lax.rem(other + 2, 4))
    parts = []
    for k, (source, row) in enumerate(zip(sources, rows)):
        to = panels.at[pl.ds(pl.multiple_of(row * count, count), count)]
        parts.append(pltpu.make_async_copy(source, to, sems.at[5 + k]))
        parts[-1].start()
    term_ref[...] = jnp.zeros_like(term_ref)

    def join(r, carry):
        at = pl.multiple_of(r * JOIN, 16)
        both = own[pl.ds(at, JOIN), :] + got[pl.ds(at, JOIN), :].astype(F32)
        nodes[pl.ds(at, JOIN), :] = both
        nodes[pl.ds(LOW + at, JOIN), :] = pltpu.roll(both, ORB, 1)
        return carry

    turns = LOW // JOIN
    gets[0].wait()
    gets[1].wait()
    lax.fori_loop(0, turns // 2, join, 0)
    gets[2].wait()
    gets[3].wait()
    lax.fori_loop(turns // 2, turns, join, 0)
    gets[4].wait()
    come = jnp.where(inner, edge[...].astype(F32), 0.0)
    ghosts[:HALF_GHOST, :] = come
    ghosts[HALF_GHOST:, :] = pltpu.roll(come, ORB, 1)
    count = GHOST // PICK_TURNS

    def add(t, carry):
        for p in range(0, count, PICKS):
            at = t * count + p
            to = [bound_ref[at + j] for j in range(PICKS)]
            base = pl.multiple_of(at, 16)
            sums = [nodes[pl.ds(i, 1), :] + ghosts[pl.ds(base + j, 1), :] for j, i in enumerate(to)]
            for i, value in zip(to, sums):
                nodes[pl.ds(i, 1), :] = value
        return carry

    lax.fori_loop(0, PICK_TURNS, add, 0)
    for copy in parts:
        copy.wait()

    puts = []
    for b in range(OWN // TURN):
        part = pl.ds(b * TURN, TURN)
        rounded = nodes[part, :].astype(BF16)
        term_ref[...] += jnp.dot(panels[:, part], rounded, preferred_element_type=F32)
        turned[:, part] = rounded.T[:ORB, :]
        puts.append(pltpu.make_async_copy(turned.at[:, part], applied_ref.at[:, part], sems.at[9 + b]))
        puts[-1].start()
    for copy in puts:
        copy.wait()


def finish(boundary, own, got, edge, panels, far, side):
    return pl.pallas_call(
        finish_kernel,
        out_shape=(jax.ShapeDtypeStruct((ORB, OWN), BF16), jax.ShapeDtypeStruct((PANELS, 128), F32)),
        in_specs=[SMEM, ANY, ANY, ANY, ANY, ANY, ANY],
        out_specs=(ANY, VMEM),
        scratch_shapes=[
            pltpu.VMEM((LOW, 128), F32),
            pltpu.VMEM((LOW, 128), BF16),
            pltpu.VMEM((HALF_GHOST, 128), BF16),
            pltpu.VMEM((PANELS, OWN), BF16),
            pltpu.VMEM((2 * LOW, 128), F32),
            pltpu.VMEM((GHOST, 128), F32),
            pltpu.VMEM((ORB, OWN), BF16),
            pltpu.SemaphoreType.DMA((9 + OWN // TURN,)),
        ],
        compiler_params=pltpu.CompilerParams(vmem_limit_bytes=VMEM_LIMIT),
    )(boundary, own, got, edge, panels, far, side)


PLANE = 16


def total_kernel(term_ref, out_ref, far, near, held, far_s, far_r, near_s, near_r):
    cell = lax.axis_index("cell")
    z, q = cell // PLANE, lax.rem(cell, PLANE)
    above = [lax.rem(z + d, 4) for d in range(1, 4)]
    beside = [lax.rem(q + d, PLANE) for d in range(1, PLANE)]
    columns = [{"cell": to * PLANE + q} for to in above]
    plane = [{"cell": z * PLANE + to} for to in beside]
    greet(columns + plane, len(columns) + len(plane))
    started = []
    for d, (to, device) in enumerate(zip(above, columns)):
        started.append(remote(term_ref.at[to], far.at[d], far_s.at[d], far_r.at[d], device))
        started[-1].start()
    for copy in started:
        copy.wait_recv()
    some = term_ref[z] + (far[0] + far[1] + far[2])
    for k in range(PLANE):
        held[k] = some[2 * k : 2 * k + 2]
    wide = []
    for d, (to, device) in enumerate(zip(beside, plane)):
        wide.append(remote(held.at[to], near.at[d], near_s.at[d], near_r.at[d], device))
        wide[-1].start()
    for copy in wide:
        copy.wait_recv()
    out_ref[...] = (held[q] + jnp.sum(near[...], axis=0))[:, :ORB]
    for copy in started + wide:
        copy.wait_send()


def total(terms):
    return pl.pallas_call(
        total_kernel,
        out_shape=jax.ShapeDtypeStruct((2, ORB), F32),
        in_specs=[VMEM],
        out_specs=VMEM,
        scratch_shapes=[
            pltpu.VMEM((3, 32, 128), F32),
            pltpu.VMEM((PLANE - 1, 2, 128), F32),
            pltpu.VMEM((PLANE, 2, 128), F32),
            pltpu.SemaphoreType.DMA((3,)),
            pltpu.SemaphoreType.DMA((3,)),
            pltpu.SemaphoreType.DMA((PLANE - 1,)),
            pltpu.SemaphoreType.DMA((PLANE - 1,)),
        ],
        compiler_params=pltpu.CompilerParams(collective_id=2, has_side_effects=True, vmem_limit_bytes=VMEM_LIMIT),
    )(terms)


def shards(orbitals, panels, stiffness, potential, connectivity, boundary):
    table = collect(orbitals, boundary)
    panels, table = lax.optimization_barrier((panels, table))
    far = lax.ppermute(panels, "orb", [(0, 2), (2, 0), (1, 3), (3, 1)])
    own, leave = elements(connectivity, potential, stiffness, table)
    got, edge, side = swap(own, leave, panels, far)
    applied, term = finish(boundary, own, got, edge, panels, far, side)
    return applied, total(term.reshape(4, PANELS // 4, 128))


def solution(mesh):
    return jax.shard_map(
        shards,
        mesh=mesh,
        in_specs=(
            P("orb", "cell"),
            P("orb", "cell"),
            P(),
            P(None, "cell"),
            P(None, "cell"),
            P("cell"),
        ),
        out_specs=(P("orb", "cell"), P("cell", "orb")),
        check_vma=False,
    )
```
